32 devices in a mesh: group: 2 (over x), dp: 8 (over z, y), basis: 2 (over core).
Axes of the slice: x: 2, y: 2, z: 4, core: 2. Of those that a mesh axis runs over, the one named last changes fastest.
Arguments:
- activations: bfloat16 [16, 256, 8192], P(('group', 'dp'), None, 'basis'), parts along dimension 0, may hold values from -6 to 6
- out_grads: bfloat16 [16, 256, 28672], P(('group', 'dp'), None, 'basis'), parts along dimension 0, may hold values from -6 to 6
- input_basis: bfloat16 [8192, 384], P('basis', 'dp'), may hold values from -0.0625 to 0.0625
- output_basis: bfloat16 [28672, 384], P('basis', 'dp'), may hold values from -0.03125 to 0.03125
Outputs:
- eigenvalues: float32 [768, 384], P(('group', 'dp', 'basis')), parts along dimension 0
The draws below stay inside these ranges and needn't reach their ends.
There are 2 independent parts, one for each index of `group`. The reference program is written for one: setup_inputs(seed, part) draws one part's arguments, and reference() takes and returns one part's arrays. A program takes and returns all parts, laid end to end along the dimension named above; an argument that names none is the same for every part. Nothing has to cross between parts.
All inputs are finite; a program needn't handle non-finite values.
Results may differ from the reference program's by a relative error of at most 0.0028.
Values may be sent and summed in bfloat16 or wider, within the bound.
No kernel may reach another device: no remote copies, remote signals or barrier semaphores. Data moves between devices by JAX's collectives and lax.ppermute only.
A program may use at most 128 MiB of HBM per device.

```python
import jax
import jax.numpy as jnp
from jax import lax

D = 8192
FF = 28672
TOK = 256
K = 384
EXAMPLES = 8


def level_of(stream_key, dims, cuts, smallest, high):
    level, own = 1.0, jax.random.fold_in(stream_key, 6)
    for position, blocks in cuts:
        draws = jnp.exp(jax.random.uniform(jax.random.fold_in(own, position), (blocks,), jnp.float32, smallest / len(cuts), high / len(cuts)))
        level = level * jnp.repeat(draws, dims[position] // blocks).reshape([-1 if axis == position else 1 for axis in range(len(dims))])
    return level


def centred(stream_key, shape, spread, bound, cuts=(), held_as=jnp.bfloat16):
    drawn = spread * jax.random.normal(stream_key, shape, jnp.float32)
    if cuts:
        drawn = drawn * level_of(stream_key, shape, cuts, -0.22, 0.18)
    return jnp.clip(drawn, -bound, bound).astype(held_as)


def setup_inputs(seed: int = 0, part: int = 0) -> dict:
    keys = jax.random.split(jax.random.key(seed), 5)
    part_keys = jax.random.split(jax.random.fold_in(keys[4], part), 5)
    return {
        "activations": centred(part_keys[0], (EXAMPLES, TOK, D), 1.0, 6.0, ((0, 8), (2, 2))),
        "out_grads": centred(part_keys[1], (EXAMPLES, TOK, FF), 1.0, 6.0, ((0, 8), (2, 2))),
        "input_basis": centred(keys[2], (D, K), D ** -0.5, 0.0625, ((0, 2), (1, 8))),
        "output_basis": centred(keys[3], (FF, K), FF ** -0.5, 0.03125, ((0, 2), (1, 8))),
    }


def reference(activations, out_grads, input_basis, output_basis):

    def one_example(pair):
        acts, grads = pair
        rot_in = jnp.dot(acts, input_basis, preferred_element_type=jnp.float32).astype(jnp.bfloat16)
        rot_out = jnp.dot(grads, output_basis, preferred_element_type=jnp.float32).astype(jnp.bfloat16)
        coeff = lax.dot_general(rot_out, rot_in, (((0,), (0,)), ((), ())), preferred_element_type=jnp.float32)
        coeff = coeff / jnp.sqrt(jnp.float32(TOK))
        return coeff * coeff
    squares = lax.map(one_example, (activations, out_grads))
    return lax.optimization_barrier(jnp.sum(squares, axis=0)) / jnp.float32(EXAMPLES)
```

```python
import functools

import jax
import jax.numpy as jnp
from jax import lax
from jax.experimental import pallas as pl
from jax.experimental.pallas import tpu as pltpu
from jax.sharding import PartitionSpec as P

TOK = 256
K = 384
LANES = 128


def place_cols(left, piece):
    product = jnp.dot(left, piece, preferred_element_type=jnp.float32)
    return product


def per_device_any(activations, out_grads, input_basis, output_basis):
    acts = activations[0]
    grads = out_grads[0]
    tokens = acts.shape[0]
    part_in = place_cols(acts, lax.all_gather(input_basis, "dp", axis=1, tiled=True))
    part_out = place_cols(grads, lax.all_gather(output_basis, "dp", axis=1, tiled=True))
    rot_in = lax.psum(part_in, "basis").astype(jnp.bfloat16)
    data_count = lax.axis_size("dp")
    panel_count = lax.axis_size("basis")
    block = K // (data_count * panel_count)
    ordered = part_out.reshape(tokens, data_count, panel_count, block)
    ordered = jnp.transpose(ordered, (0, 2, 1, 3)).reshape(tokens, K)
    rot_out = lax.psum_scatter(ordered, "basis", scatter_dimension=1, tiled=True).astype(
        jnp.bfloat16
    )
    coeff = lax.dot_general(
        rot_out, rot_in, (((0,), (0,)), ((), ())), preferred_element_type=jnp.float32
    )
    coeff = coeff / jnp.sqrt(jnp.float32(TOK))
    summed = lax.psum_scatter(coeff * coeff, "dp", scatter_dimension=0, tiled=True)
    return summed / jnp.float32(data_count)


def nt_dot(left, right):
    return lax.dot_general(
        left, right, (((1,), (1,)), ((), ())), preferred_element_type=jnp.float32
    )


def rotate_kernel(plan, where_ref, acts_ref, grads_ref, *refs):
    in_half, out_half, chunks = plan
    out_ref = refs[-1]
    own, other, tail = refs[0 : 2 * len(chunks)], refs[2 * len(chunks) : -2], refs[-2]
    x, core = where_ref[0], where_ref[1]
    rows = own[0].shape[0]
    rot_in = jnp.zeros((2 * rows, acts_ref.shape[0]), jnp.float32)
    rot_out = rot_in
    for side, pieces in ((x, own), (1 - x, other)):
        in_at, out_at = 0, 0
        for c, (in_w, out_w) in enumerate(chunks):
            both = jnp.concatenate([pieces[2 * c][...], pieces[2 * c + 1][...]], axis=0)
            if in_w:
                cols = pl.ds(pl.multiple_of(side * in_half + in_at, LANES), in_w)
                rot_in += nt_dot(both[:, :in_w], acts_ref[:, cols])
                in_at += in_w
            if out_w:
                cols = pl.ds(pl.multiple_of(side * out_half + out_at, LANES), out_w)
                rot_out += nt_dot(both[:, in_w:], grads_ref[:, cols])
                out_at += out_w
    rot_out += nt_dot(tail[...], grads_ref[:, 2 * out_half :])
    half = rows // 2
    out_ref[0, : 2 * rows] = rot_in
    out_ref[1, : 2 * rows] = rot_in
    for shard in range(2):
        first = rot_out[shard * rows : shard * rows + half]
        second = rot_out[shard * rows + half : (shard + 1) * rows]
        at = pl.ds(2 * rows + shard * half, half)
        out_ref[0, at] = jnp.where(core == 0, first, second)
        out_ref[1, at] = jnp.where(core == 0, second, first)


def finish_kernel(rows, where_ref, *refs):
    count = 4
    keep, come = refs[:count], refs[count : 2 * count]
    outs = refs[2 * count : -2]
    in_ref, out_ref = refs[-2:]
    half = rows // 2
    for slot in range(count):
        total = keep[slot][...] + come[slot][...]
        for shard in range(2):
            owner = where_ref[2 * slot + shard]
            at = pl.ds(pl.multiple_of(owner * rows, 16), rows)
            in_ref[at, :] = total[shard * rows : (shard + 1) * rows].astype(jnp.bfloat16)
            place = where_ref[2 * count + 2 * slot + shard]
            at = pl.ds(pl.multiple_of(place * half, 8), half)
            begin = 2 * rows + shard * half
            out_ref[at, :] = total[begin : begin + half]
    coeff = nt_dot(out_ref[...].astype(jnp.bfloat16), in_ref[...])
    coeff = coeff * (1.0 / TOK**0.5)
    square = coeff * coeff
    for place, ref in enumerate(outs):
        ref[...] = square[place * half : (place + 1) * half]


def per_device_plane(activations, out_grads, input_basis, output_basis):
    acts, grads = activations[0], out_grads[0]
    in_t, out_t = input_basis.T, output_basis.T
    rows = in_t.shape[0]
    tokens = acts.shape[0]
    x = lax.axis_index("group")
    me = lax.axis_index("dp")
    core = lax.axis_index("basis")
    z, y = me // 2, me % 2
    middle = (z == 1) | (z == 2)

    in_half = in_t.shape[1] // 2
    out_half = out_t.shape[1] * 3 // 8
    width = (in_half + out_half) // 2
    width = -(-width // 256) * 256
    chunks = ((in_half, width - in_half), (0, out_half - width + in_half))

    def along(pairs):
        return [(2 * a + b, 2 * c + b) for a, c in pairs for b in range(2)]

    def shift(value, pairs):
        return lax.ppermute(value, "dp", along(pairs))

    def swap_y(value):
        return lax.ppermute(value, "dp", [(i, i ^ 1) for i in range(8)])

    def swap_x(value):
        return lax.ppermute(value, "group", [(0, 1), (1, 0)])

    def share(side):
        ins = lax.dynamic_slice_in_dim(in_t, side * in_half, in_half, 1)
        outs = lax.dynamic_slice_in_dim(out_t, side * out_half, out_half, 1)
        cut = chunks[0][1]
        return [jnp.concatenate([ins, outs[:, :cut]], axis=1), outs[:, cut:]]

    def line(value):
        left = shift(value, [(1, 0), (2, 1), (3, 2)])
        right = shift(value, [(0, 1), (1, 2), (2, 3)])
        ends = shift(jnp.where(z == 1, left, right), [(1, 0), (2, 3)])
        mids = shift(jnp.where(z == 2, left, right), [(2, 1), (1, 2)])
        last = shift(mids, [(1, 0), (2, 3)])
        return (
            jnp.where(z == 3, right, left),
            jnp.where(middle, right, ends),
            jnp.where(middle, mids, last),
        )

    mine = share(x)
    theirs = share(1 - x)
    tail = out_t[:, 2 * out_half :]
    other_y = [swap_y(c) for c in mine]
    tails = jnp.concatenate([tail, swap_y(tail)], axis=0)
    both = [swap_x(c) for c in other_y]

    groups = [(mine, other_y, theirs, both)]
    lines = [line(c) for c in mine]
    for slot in range(3):
        have = [chunk[slot] for chunk in lines]
        by_y = [swap_y(c) for c in have]
        by_x = [swap_x(c) for c in have]
        far = [swap_x(by_y[0]), swap_y(by_x[1])]
        groups.append((have, by_y, by_x, far))
    tails = [tails, *line(tails)]

    plan = (in_half, out_half, chunks)
    place = jnp.stack([x, core]).astype(jnp.int32)
    vmem = pl.BlockSpec(memory_space=pltpu.VMEM)
    keeps, sends = [], []
    for (have, by_y, by_x, far), end in zip(groups, tails):
        flat = [v for pair in zip(have, by_y) for v in pair]
        flat += [v for pair in zip(by_x, far) for v in pair]
        got = pl.pallas_call(
            functools.partial(rotate_kernel, plan),
            out_shape=jax.ShapeDtypeStruct((2, 3 * rows, tokens), jnp.float32),
            in_specs=[pl.BlockSpec(memory_space=pltpu.SMEM)] + [vmem] * (len(flat) + 3),
            out_specs=vmem,
            compiler_params=pltpu.CompilerParams(vmem_limit_bytes=40 * 2**20),
            cost_estimate=pl.CostEstimate(
                flops=4 * rows * tokens * (acts.shape[1] + grads.shape[1]),
                bytes_accessed=2 * (tokens + 2 * rows) * (acts.shape[1] + grads.shape[1]),
                transcendentals=0,
            ),
            name="rotate",
        )(place, acts, grads, *flat, end)
        keeps.append(got[0])
        sends.append(got[1])
    comes = [lax.ppermute(s, "basis", [(0, 1), (1, 0)]) for s in sends]

    order = jnp.array([[0, 1, 2, 3], [1, 2, 0, 3], [2, 3, 1, 0], [3, 2, 1, 0]], jnp.int32)[z]
    owners = jnp.stack([order * 2 + y, order * 2 + 1 - y], axis=1).reshape(-1)
    table = jnp.concatenate([owners, owners ^ me]).astype(jnp.int32)
    squares = pl.pallas_call(
        functools.partial(finish_kernel, rows),
        out_shape=[jax.ShapeDtypeStruct((rows // 2, K), jnp.float32)] * 8,
        in_specs=[pl.BlockSpec(memory_space=pltpu.SMEM)] + [vmem] * 8,
        out_specs=[vmem] * 8,
        scratch_shapes=[
            pltpu.VMEM((K, tokens), jnp.bfloat16),
            pltpu.VMEM((K // 2, tokens), jnp.float32),
        ],
        name="finish",
    )(table, *keeps, *comes)
    total = squares[0]
    for k in range(1, 8):
        total = total + lax.ppermute(squares[k], "dp", [(i, i ^ k) for i in range(8)])
    return total * (1.0 / 8)


def solution(mesh):
    in_specs = (
        P(("group", "dp"), None, "basis"),
        P(("group", "dp"), None, "basis"),
        P("basis", "dp"),
        P("basis", "dp"),
    )
    out_specs = P(("group", "dp", "basis"), None)
    plane = (mesh.shape["group"], mesh.shape["dp"], mesh.shape["basis"]) == (2, 8, 2)
    return jax.shard_map(
        per_device_plane if plane else per_device_any,
        mesh=mesh,
        in_specs=in_specs,
        out_specs=out_specs,
        check_vma=False,
    )
```

```python
import functools

import jax
import jax.numpy as jnp
from jax import lax
from jax.experimental import pallas as pl
from jax.experimental.pallas import tpu as pltpu
from jax.sharding import PartitionSpec as P

TOK = 256
K = 384
LANES = 128


def place_cols(left, piece):
    product = jnp.dot(left, piece, preferred_element_type=jnp.float32)
    return product


def per_device_any(activations, out_grads, input_basis, output_basis):
    acts = activations[0]
    grads = out_grads[0]
    tokens = acts.shape[0]
    part_in = place_cols(acts, lax.all_gather(input_basis, "dp", axis=1, tiled=True))
    part_out = place_cols(grads, lax.all_gather(output_basis, "dp", axis=1, tiled=True))
    rot_in = lax.psum(part_in, "basis").astype(jnp.bfloat16)
    data_count = lax.axis_size("dp")
    panel_count = lax.axis_size("basis")
    block = K // (data_count * panel_count)
    ordered = part_out.reshape(tokens, data_count, panel_count, block)
    ordered = jnp.transpose(ordered, (0, 2, 1, 3)).reshape(tokens, K)
    rot_out = lax.psum_scatter(ordered, "basis", scatter_dimension=1, tiled=True).astype(
        jnp.bfloat16
    )
    coeff = lax.dot_general(
        rot_out, rot_in, (((0,), (0,)), ((), ())), preferred_element_type=jnp.float32
    )
    coeff = coeff / jnp.sqrt(jnp.float32(TOK))
    summed = lax.psum_scatter(coeff * coeff, "dp", scatter_dimension=0, tiled=True)
    return summed / jnp.float32(data_count)


def nt_dot(left, right):
    return lax.dot_general(
        left, right, (((1,), (1,)), ((), ())), preferred_element_type=jnp.float32
    )


def cut_kernel(in_half, first, in_ref, out_ref, m0, m1, t0, t1):
    x = lax.axis_index("group")
    out_half = first + m1.shape[1]
    for side, unit0, unit1 in ((x, m0, m1), (1 - x, t0, t1)):
        in_at = pl.multiple_of(side * in_half, LANES)
        out_at = pl.multiple_of(side * out_half, LANES)
        next_at = pl.multiple_of(side * out_half + first, LANES)
        unit0[:, :in_half] = in_ref[:, pl.ds(in_at, in_half)]
        unit0[:, in_half:] = out_ref[:, pl.ds(out_at, first)]
        unit1[...] = out_ref[:, pl.ds(next_at, unit1.shape[1])]


def rotate_kernel(plan, in_half, first, acts_ref, grads_ref, *refs):
    x = lax.axis_index("group")
    core = lax.axis_index("basis")
    terms, has_acc, last = plan
    refs = list(refs)
    out_half = grads_ref.shape[1] // 2
    rot_in = rot_out = None
    for mine, index, count in terms:
        pieces, refs = refs[:count], refs[count:]
        rows = jnp.concatenate([p[...] for p in pieces], axis=0)
        side = x if mine else 1 - x
        if index == 0:
            cols = pl.ds(pl.multiple_of(side * in_half, LANES), in_half)
            part = nt_dot(rows[:, :in_half], acts_ref[:, cols])
            rot_in = part if rot_in is None else rot_in + part
            cols = pl.ds(pl.multiple_of(side * out_half, LANES), first)
            part = nt_dot(rows[:, in_half:], grads_ref[:, cols])
        else:
            cols = pl.ds(pl.multiple_of(side * out_half + first, LANES), out_half - first)
            part = nt_dot(rows, grads_ref[:, cols])
        rot_out = part if rot_out is None else rot_out + part
    if has_acc:
        if rot_in is not None:
            rot_in += refs.pop(0)[...]
        rot_out += refs.pop(0)[...]
    if rot_in is not None:
        refs.pop(0)[...] = rot_in
    if not last:
        refs.pop(0)[...] = rot_out
        return
    keep, send = refs
    panel = pieces[0].shape[0] // 2
    for shard in range(rot_out.shape[0] // (2 * panel)):
        low = rot_out[2 * shard * panel : (2 * shard + 1) * panel]
        high = rot_out[(2 * shard + 1) * panel : 2 * (shard + 1) * panel]
        at = slice(shard * panel, (shard + 1) * panel)
        keep[at] = jnp.where(core == 0, low, high)
        send[at] = jnp.where(core == 0, high, low)


def finish_kernel(rows, table_ref, *refs):
    ins, keep, come = refs[0:4], refs[4:6], refs[6:8]
    outs = refs[8:-2]
    in_ref, out_ref = refs[-2:]
    half = rows // 2
    for shard in range(8):
        part, local = (0, shard) if shard < 2 else (1, shard - 2)
        owner = table_ref[shard]
        block = ins[2 * part][pl.ds(local * rows, rows)] + ins[2 * part + 1][pl.ds(local * rows, rows)]
        in_ref[pl.ds(pl.multiple_of(owner * rows, 16), rows), :] = block.astype(jnp.bfloat16)
        place = table_ref[8 + shard]
        at = pl.ds(local * half, half)
        out_ref[pl.ds(pl.multiple_of(place * half, 8), half), :] = keep[part][at] + come[part][at]
    coeff = nt_dot(out_ref[...].astype(jnp.bfloat16), in_ref[...])
    coeff = coeff * (1.0 / TOK**0.5)
    square = coeff * coeff
    for place, ref in enumerate(outs):
        ref[...] = square[place * half : (place + 1) * half]


def per_device_plane(activations, out_grads, input_basis, output_basis):
    acts, grads = activations[0], out_grads[0]
    in_t, out_t = input_basis.T, output_basis.T
    rows = in_t.shape[0]
    tokens = acts.shape[0]
    me = lax.axis_index("dp")
    z, y = me // 2, me % 2
    in_half = in_t.shape[1] // 2
    width = (in_t.shape[1] + out_t.shape[1]) // 4
    first = width - in_half

    vmem = pl.BlockSpec(memory_space=pltpu.VMEM)

    def shift(value, pairs):
        return lax.ppermute(value, "dp", [(2 * a + b, 2 * c + b) for a, c in pairs for b in range(2)])

    def swap_y(value):
        return lax.ppermute(value, "dp", [(i, i ^ 1) for i in range(8)])

    def swap_x(value):
        return lax.ppermute(value, "group", [(0, 1), (1, 0)])

    def swap_core(value):
        return lax.ppermute(value, "basis", [(0, 1), (1, 0)])

    def by_z(*choices):
        out = choices[3]
        for i in (2, 1, 0):
            if choices[i] is not out:
                out = jnp.where(z <= i, choices[i], out)
        return out

    unit = jax.ShapeDtypeStruct((rows, width), in_t.dtype)
    m0, m1, t0, t1 = pl.pallas_call(
        functools.partial(cut_kernel, in_half, first),
        out_shape=[unit] * 4,
        in_specs=[vmem] * 2,
        out_specs=[vmem] * 4,
        name="cut",
    )(in_t, out_t)

    down = [(1, 0), (2, 1), (3, 2)]
    up = [(0, 1), (1, 2), (2, 3)]
    L, R = {}, {}
    held = [{}, {}, {}, {}]
    own, one, two, three = held
    own.update(m0=m0, m1=m1, t0=t0, t1=t1)

    def settle(r):
        names = [(h, k) for h in held for k in h]
        sides = [(d, k) for d in (L, R) for k in d if k < r - 1]
        values = [h[k] for h, k in names + sides]
        for (h, k), v in zip(names + sides, lax.optimization_barrier(tuple(values))):
            h[k] = v

    def both_ways(r, at_end, count=3):
        a, b = (m0, m0) if r == 1 else (m1, m1) if r == 2 else (L[r - 2], R[r - 2])
        if at_end is not None:
            a, b = jnp.where(z == 3, at_end, a), jnp.where(z == 0, at_end, b)
        L[r], R[r] = shift(a, down[:count]), shift(b, up[3 - count :])

    def ends(r):
        L[r] = R[r] = shift(jnp.where(z == 1, L[r - 2], R[r - 2]), [(1, 0), (2, 3)])

    plan_y = ["", "0om0", "0om1", "1om0", "1om1", "2om0", "2om1", "3om0", "2ot0", "3ot0", "1ot1"]
    plan_x = ["", "", "", "0ot0", "0ot1", "1t1", "2t0", "1t0", "1ot0", "2t1", "2ot1"]
    at_end = {3: "t0", 4: "t1", 5: "om1", 6: "ot1"}
    other = {"m": "t", "t": "m"}
    waiting = {}
    for r in range(1, 11):
        if r > 2:
            for h, k, v in waiting.pop(r - 2):
                h[k] = v
            settle(r)
        for i, (slot, name) in enumerate(((one, "m0"), (one, "m1"))):
            if r == 3 + i:
                slot[name] = by_z(L[1 + i], L[1 + i], R[1 + i], R[1 + i])
        for i, name in enumerate(("m0", "m1")):
            if r == 5 + i:
                two[name] = by_z(L[3 + i], R[1 + i], L[1 + i], R[3 + i])
        for i, name in enumerate(("m0", "m1", "t0", "t1")):
            if r == 7 + i:
                three[name] = by_z(L[5 + i], L[3 + i], R[3 + i], R[5 + i])
        if r < 9:
            both_ways(r, own[at_end[r]] if r in at_end else None, 3 if r < 7 else 2)
        else:
            ends(r)
        waiting[r] = []
        name = plan_y[r]
        slot = held[int(name[0])]
        waiting[r].append((slot, name[1:], swap_y(slot[name[2:]])))
        if plan_x[r]:
            name = plan_x[r]
            slot = held[int(name[0])]
            source = name[1:-2] + other[name[-2]] + name[-1]
            waiting[r].append((slot, name[1:], swap_x(slot[source])))
    for r in (9, 10):
        for h, k, v in waiting.pop(r):
            h[k] = v
    three["om1"] = by_z(L[9], L[7], R[7], R[9])
    three["ot1"] = by_z(L[10], L[8], R[8], R[10])

    def rotate(slots, names, acc, last):
        terms, pieces, out_shape = [], [], []
        count = 2 * len(slots)
        for name in names:
            terms.append((name[0] == "m", int(name[1]), count))
            pieces += [v for s in slots for v in (s[name], s["o" + name])]
        full = jax.ShapeDtypeStruct((count * rows, tokens), jnp.float32)
        panel = jax.ShapeDtypeStruct((count * rows // 2, tokens), jnp.float32)
        if any(name[1] == "0" for name in names):
            out_shape.append(full)
        out_shape += [panel, panel] if last else [full]
        return pl.pallas_call(
            functools.partial(rotate_kernel, (terms, bool(acc), last), in_half, first),
            out_shape=out_shape,
            in_specs=[vmem] * (2 + len(pieces) + len(acc)),
            out_specs=[vmem] * len(out_shape),
            compiler_params=pltpu.CompilerParams(vmem_limit_bytes=40 * 2**20),
            cost_estimate=pl.CostEstimate(
                flops=2 * len(pieces) * rows * width * tokens,
                bytes_accessed=2 * len(pieces) * rows * width,
                transcendentals=0,
            ),
            name="rotate",
        )(acts, grads, *pieces, *acc)

    in_a, keep_a, send_a = rotate([own], ["m0", "m1", "t0", "t1"], [], True)
    rest = [one, two, three]
    acc = rotate(rest, ["m0"], [], False)
    in_b, acc_out = rotate(rest, ["m1", "t0"], acc, False)
    keep_b, send_b = rotate(rest, ["t1"], [acc_out], True)

    order = jnp.array([[0, 1, 2, 3], [1, 2, 0, 3], [2, 1, 3, 0], [3, 2, 1, 0]], jnp.int32)[z]
    owners = jnp.stack([order * 2 + y, order * 2 + 1 - y], axis=1).reshape(-1)
    table = jnp.concatenate([owners, owners ^ me]).astype(jnp.int32)
    squares = pl.pallas_call(
        functools.partial(finish_kernel, rows),
        out_shape=[jax.ShapeDtypeStruct((rows // 2, K), jnp.float32)] * 8,
        in_specs=[pl.BlockSpec(memory_space=pltpu.SMEM)] + [vmem] * 8,
        out_specs=[vmem] * 8,
        scratch_shapes=[
            pltpu.VMEM((K, tokens), jnp.bfloat16),
            pltpu.VMEM((K // 2, tokens), jnp.float32),
        ],
        name="finish",
    )(
        table, in_a, swap_core(in_a), in_b, swap_core(in_b),
        keep_a, keep_b, swap_core(send_a), swap_core(send_b),
    )
    total = squares[0]
    for k in range(1, 8):
        total = total + lax.ppermute(squares[k], "dp", [(i, i ^ k) for i in range(8)])
    return total * (1.0 / 8)


def solution(mesh):
    in_specs = (
        P(("group", "dp"), None, "basis"),
        P(("group", "dp"), None, "basis"),
        P("basis", "dp"),
        P("basis", "dp"),
    )
    out_specs = P(("group", "dp", "basis"), None)
    plane = (mesh.shape["group"], mesh.shape["dp"], mesh.shape["basis"]) == (2, 8, 2)
    return jax.shard_map(
        per_device_plane if plane else per_device_any,
        mesh=mesh,
        in_specs=in_specs,
        out_specs=out_specs,
        check_vma=False,
    )
```

```python
import functools

import jax
import jax.numpy as jnp
from jax import lax
from jax.experimental import pallas as pl
from jax.experimental.pallas import tpu as pltpu
from jax.sharding import PartitionSpec as P

TOK = 256
K = 384
LANES = 128
AHEAD = 5


def place_cols(left, piece):
    product = jnp.dot(left, piece, preferred_element_type=jnp.float32)
    return product


def per_device_any(activations, out_grads, input_basis, output_basis):
    acts = activations[0]
    grads = out_grads[0]
    tokens = acts.shape[0]
    part_in = place_cols(acts, lax.all_gather(input_basis, "dp", axis=1, tiled=True))
    part_out = place_cols(grads, lax.all_gather(output_basis, "dp", axis=1, tiled=True))
    rot_in = lax.psum(part_in, "basis").astype(jnp.bfloat16)
    data_count = lax.axis_size("dp")
    panel_count = lax.axis_size("basis")
    block = K // (data_count * panel_count)
    ordered = part_out.reshape(tokens, data_count, panel_count, block)
    ordered = jnp.transpose(ordered, (0, 2, 1, 3)).reshape(tokens, K)
    rot_out = lax.psum_scatter(ordered, "basis", scatter_dimension=1, tiled=True).astype(
        jnp.bfloat16
    )
    coeff = lax.dot_general(
        rot_out, rot_in, (((0,), (0,)), ((), ())), preferred_element_type=jnp.float32
    )
    coeff = coeff / jnp.sqrt(jnp.float32(TOK))
    summed = lax.psum_scatter(coeff * coeff, "dp", scatter_dimension=0, tiled=True)
    return summed / jnp.float32(data_count)


def nt_dot(left, right):
    return lax.dot_general(
        left, right, (((1,), (1,)), ((), ())), preferred_element_type=jnp.float32
    )


def cut_kernel(in_half, first, in_ref, out_ref, m0, m1, t0, t1):
    x = lax.axis_index("group")
    out_half = first + m1.shape[1]
    for side, unit0, unit1 in ((x, m0, m1), (1 - x, t0, t1)):
        in_at = pl.multiple_of(side * in_half, LANES)
        out_at = pl.multiple_of(side * out_half, LANES)
        next_at = pl.multiple_of(side * out_half + first, LANES)
        unit0[:, :in_half] = in_ref[:, pl.ds(in_at, in_half)]
        unit0[:, in_half:] = out_ref[:, pl.ds(out_at, first)]
        unit1[...] = out_ref[:, pl.ds(next_at, unit1.shape[1])]


def rotate_kernel(plan, in_half, first, acts_ref, grads_ref, *refs):
    x = lax.axis_index("group")
    core = lax.axis_index("basis")
    terms, has_acc, last = plan
    refs = list(refs)
    stack = refs.pop()
    z = lax.axis_index("dp") // 2
    outer = (z == 0) | (z == 3)
    out_half = grads_ref.shape[1] // 2
    rot_in = rot_out = None
    for mine, index, pieces in terms:
        rows = refs[0].shape[0]
        for i, (at_outer, at_inner) in enumerate(pieces):
            at = slice(i * rows, (i + 1) * rows)
            if at_outer == at_inner:
                stack[at] = refs[at_outer][...]
                continue

            @pl.when(outer)
            def _():
                stack[at] = refs[at_outer][...]

            @pl.when(jnp.logical_not(outer))
            def _():
                stack[at] = refs[at_inner][...]

        side = x if mine else 1 - x
        if index == 0:
            cols = pl.ds(pl.multiple_of(side * in_half, LANES), in_half)
            part = nt_dot(stack[:, :in_half], acts_ref[:, cols])
            rot_in = part if rot_in is None else rot_in + part
            cols = pl.ds(pl.multiple_of(side * out_half, LANES), first)
            part = nt_dot(stack[:, in_half:], grads_ref[:, cols])
        else:
            cols = pl.ds(pl.multiple_of(side * out_half + first, LANES), out_half - first)
            part = nt_dot(stack[...], grads_ref[:, cols])
        rot_out = part if rot_out is None else rot_out + part
    panel = refs[0].shape[0] // 2
    refs = refs[1 + max(i for term in terms for pair in term[2] for i in pair) :]
    if has_acc:
        if rot_in is not None:
            rot_in += refs.pop(0)[...]
        rot_out += refs.pop(0)[...]
    if rot_in is not None:
        refs.pop(0)[...] = rot_in
    if not last:
        refs.pop(0)[...] = rot_out
        return
    keep, send = refs
    for shard in range(rot_out.shape[0] // (2 * panel)):
        low = rot_out[2 * shard * panel : (2 * shard + 1) * panel]
        high = rot_out[(2 * shard + 1) * panel : 2 * (shard + 1) * panel]
        at = slice(shard * panel, (shard + 1) * panel)
        keep[at] = jnp.where(core == 0, low, high)
        send[at] = jnp.where(core == 0, high, low)


def finish_kernel(rows, *refs):
    me = lax.axis_index("dp")
    z, y = me // 2, me % 2
    order = [z]
    for by_z in ((1, 2, 1, 2), (2, 0, 3, 1), (3, 3, 0, 0)):
        order.append(jnp.where(z == 0, by_z[0], jnp.where(z == 1, by_z[1], jnp.where(z == 2, by_z[2], by_z[3]))))
    ins, keep, come = refs[0:4], refs[4:6], refs[6:8]
    outs = refs[8:-2]
    in_ref, out_ref = refs[-2:]
    half = rows // 2
    for shard in range(8):
        part, local = (0, shard) if shard < 2 else (1, shard - 2)
        owner = order[shard // 2] * 2 + (y if shard % 2 == 0 else 1 - y)
        block = ins[2 * part][pl.ds(local * rows, rows)] + ins[2 * part + 1][pl.ds(local * rows, rows)]
        in_ref[pl.ds(pl.multiple_of(owner * rows, 16), rows), :] = block.astype(jnp.bfloat16)
        place = owner ^ me
        at = pl.ds(local * half, half)
        out_ref[pl.ds(pl.multiple_of(place * half, 8), half), :] = keep[part][at] + come[part][at]
    coeff = nt_dot(out_ref[...].astype(jnp.bfloat16), in_ref[...])
    coeff = coeff * (1.0 / TOK**0.5)
    square = coeff * coeff
    for place, ref in enumerate(outs):
        ref[...] = square[place * half : (place + 1) * half]


def per_device_plane(activations, out_grads, input_basis, output_basis):
    acts, grads = activations[0], out_grads[0]
    in_t, out_t = input_basis.T, output_basis.T
    rows = in_t.shape[0]
    tokens = acts.shape[0]
    me = lax.axis_index("dp")
    z, y = me // 2, me % 2
    in_half = in_t.shape[1] // 2
    width = (in_t.shape[1] + out_t.shape[1]) // 4
    first = width - in_half

    vmem = pl.BlockSpec(memory_space=pltpu.VMEM)

    def swap_core(value):
        return lax.ppermute(value, "basis", [(0, 1), (1, 0)])

    unit = jax.ShapeDtypeStruct((rows, width), in_t.dtype)
    m0, m1, t0, t1 = pl.pallas_call(
        functools.partial(cut_kernel, in_half, first),
        out_shape=[unit] * 4,
        in_specs=[vmem] * 2,
        out_specs=[vmem] * 4,
        name="cut",
    )(in_t, out_t)

    def rotate(slots, names, acc, last):
        terms, pieces, out_shape = [], [], []
        count = 2 * len(slots)

        def ref_of(value):
            for i, piece in enumerate(pieces):
                if piece is value:
                    return i
            pieces.append(value)
            return len(pieces) - 1

        for name in names:
            terms.append((name[0] == "m", int(name[1]), [
                (ref_of(at_outer[s + k]), ref_of(at_inner[s + k])) for s in slots for k in (name, "o" + name)
            ]))
        full = jax.ShapeDtypeStruct((count * rows, tokens), jnp.float32)
        panel = jax.ShapeDtypeStruct((count * rows // 2, tokens), jnp.float32)
        if any(name[1] == "0" for name in names):
            out_shape.append(full)
        out_shape += [panel, panel] if last else [full]
        return pl.pallas_call(
            functools.partial(rotate_kernel, (terms, bool(acc), last), in_half, first),
            out_shape=out_shape,
            in_specs=[vmem] * (2 + len(pieces) + len(acc)),
            out_specs=[vmem] * len(out_shape),
            scratch_shapes=[pltpu.VMEM((count * rows, width), in_t.dtype)],
            compiler_params=pltpu.CompilerParams(vmem_limit_bytes=20 * 2**20),
            cost_estimate=pl.CostEstimate(
                flops=2 * len(names) * count * rows * width * tokens,
                bytes_accessed=2 * len(pieces) * rows * width,
                transcendentals=0,
            ),
            name="rotate",
        )(acts, grads, *pieces, *acc)

    outer = (z == 0) | (z == 3)
    cells = range(8)
    link_a = [(i, i ^ 2) for i in cells]
    link_b = [(i, 2 * (3 - i // 2) + i % 2) for i in cells if 2 <= i < 6]
    link_y = [(i, i ^ 1) for i in cells]
    at_ends = [i for i in cells if i < 2 or i >= 6]

    def group_pairs(pairs):
        return [(8 * g + a, 8 * g + b) for g in range(2) for a, b in pairs]

    def across_x(where):
        return [(8 * g + i, 8 * (1 - g) + i) for g in range(2) for i in where]

    def send(value, pairs):
        return lax.ppermute(value, ("group", "dp"), pairs)

    def pick(for_outer, for_inner):
        if for_outer is for_inner:
            return for_outer
        return jnp.where(outer, for_outer, for_inner)

    at_outer = {"0m0": m0, "0m1": m1, "0t0": t0, "0t1": t1}
    at_inner = dict(at_outer)
    a_outer = ["1m0", "1m1", "2m0", "2m1", "3m0", "3m1", "3om0", "3t0", "3ot0", "3t1"]
    a_inner = ["2m0", "2m1", "2om0", "2t0", "2ot0", "2t1", "2om1", "2ot1"]
    b_inner = ["1m0", "1m1", "3m0", "3m1", "3om0", "3t0", "3ot0", "3t1", "3om1", "3ot1"]
    y_outer = ["0om0", "0om1", "1om0", "1om1", "2om0", "2om1", "1ot1", "3om1", "2ot0", "2ot1"]
    x_outer = [None, None, "0ot0", "0ot1", "1t1", "2t0", "1t0", "2t1", "1ot0", "3ot1"]
    y_inner = ["0om0", "0om1", None, None, "1om0", "1om1", None, None, None, "1ot1"]
    x_inner = [None, None, "0ot0", "0ot1", None, None, "1t0", "1t1", "1ot0", None]
    to_inner = ["0" + name[1:] for name in a_inner]

    def over_y(name):
        return name.replace("o", "")

    def over_x(name):
        return name.translate(str.maketrans("mt", "tm"))

    extra, sent = {}, []

    def settle():
        if len(sent) >= AHEAD:
            extra["sent"] = sent[-AHEAD]
        spots = [(u, k) for u in (at_outer, at_inner, extra) for k in u]
        unique = {id(u[k]): u[k] for u, k in spots}
        fresh = dict(zip(unique, lax.optimization_barrier(tuple(unique.values()))))
        for u, k in spots:
            u[k] = fresh[id(u[k])]

    def bring(value, pairs, *landings):
        got = send(value, pairs)
        sent.append(got)
        return [(units, name, got) for units, name in landings]

    landing = {}
    for r in range(1, 11):
        i = r - 1
        for units, name, value in landing.pop(r - 2, []):
            units[name] = value
        settle()
        outward = at_inner["0" + a_outer[i][1:]] if r < 3 else at_inner[b_inner[i - 2]]
        if r < 9:
            value, pairs = pick(at_outer[to_inner[i]], outward), group_pairs(link_a)
            spots = [(at_outer, a_outer[i]), (at_inner, a_inner[i])]
        else:
            value, pairs = outward, group_pairs([p for p in link_a if p[1] in at_ends])
            spots = [(at_outer, a_outer[i])]
        landing[r] = bring(value, pairs, *spots)
        settle()
        crossing = at_inner["0" + b_inner[i][1:]] if r < 3 else at_inner[a_inner[i - 2]]
        value = at_outer[over_y(y_outer[i])]
        spots = [(at_outer, y_outer[i])]
        if y_inner[i]:
            value, pairs = pick(value, at_inner[over_y(y_inner[i])]), group_pairs(link_y)
            spots.append((at_inner, y_inner[i]))
        else:
            y_pairs = [p for p in link_y if p[0] in at_ends]
            value, pairs = pick(value, crossing), group_pairs(y_pairs + link_b)
            spots.append((at_inner, b_inner[i]))
        landing[r] += bring(value, pairs, *spots)
        settle()
        if x_inner[i]:
            value = pick(at_outer[over_x(x_outer[i])], at_inner[over_x(x_inner[i])])
            spots, pairs = [(at_inner, x_inner[i])], across_x(cells)
        else:
            crossing = at_inner["0" + b_inner[i][1:]] if r < 3 else at_inner[a_inner[i - 2]]
            spots, pairs = [(at_inner, b_inner[i])], group_pairs(link_b)
            value = crossing
            if x_outer[i]:
                value = pick(at_outer[over_x(x_outer[i])], crossing)
                pairs = across_x(at_ends) + pairs
        if x_outer[i]:
            spots.append((at_outer, x_outer[i]))
        landing[r] += bring(value, pairs, *spots)
        if r == 7:
            extra["in_a"], extra["keep_a"], extra["send_a"] = rotate("0", ["m0", "m1", "t0", "t1"], [], True)
        if r == 9:
            extra["acc_in"], extra["acc_out"] = rotate("123", ["m0"], [], False)
    for r in (9, 10):
        for units, name, value in landing.pop(r):
            units[name] = value
    in_a, keep_a, send_a = extra["in_a"], extra["keep_a"], extra["send_a"]
    in_b, acc_out = rotate("123", ["t0"], [extra["acc_in"], extra["acc_out"]], False)
    (acc_out,) = rotate("123", ["m1"], [acc_out], False)
    keep_b, send_b = rotate("123", ["t1"], [acc_out], True)

    squares = pl.pallas_call(
        functools.partial(finish_kernel, rows),
        out_shape=[jax.ShapeDtypeStruct((rows // 2, K), jnp.float32)] * 8,
        in_specs=[vmem] * 8,
        out_specs=[vmem] * 8,
        scratch_shapes=[
            pltpu.VMEM((K, tokens), jnp.bfloat16),
            pltpu.VMEM((K // 2, tokens), jnp.float32),
        ],
        name="finish",
    )(
        in_a, swap_core(in_a), in_b, swap_core(in_b),
        keep_a, keep_b, swap_core(send_a), swap_core(send_b),
    )
    total = squares[0]
    for k in range(1, 8):
        total = total + lax.ppermute(squares[k], "dp", [(i, i ^ k) for i in range(8)])
    return total * (1.0 / 8)


def solution(mesh):
    in_specs = (
        P(("group", "dp"), None, "basis"),
        P(("group", "dp"), None, "basis"),
        P("basis", "dp"),
        P("basis", "dp"),
    )
    out_specs = P(("group", "dp", "basis"), None)
    plane = (mesh.shape["group"], mesh.shape["dp"], mesh.shape["basis"]) == (2, 8, 2)
    return jax.shard_map(
        per_device_plane if plane else per_device_any,
        mesh=mesh,
        in_specs=in_specs,
        out_specs=out_specs,
        check_vma=False,
    )
```

```python
import functools

import jax
import jax.numpy as jnp
from jax import lax
from jax.experimental import pallas as pl
from jax.experimental.pallas import tpu as pltpu
from jax.sharding import PartitionSpec as P

TOK = 256
K = 384
LANES = 128
AHEAD = 5
STEP = 1 * 10**8


def place_cols(left, piece):
    product = jnp.dot(left, piece, preferred_element_type=jnp.float32)
    return product


def per_device_any(activations, out_grads, input_basis, output_basis):
    acts = activations[0]
    grads = out_grads[0]
    tokens = acts.shape[0]
    part_in = place_cols(acts, lax.all_gather(input_basis, "dp", axis=1, tiled=True))
    part_out = place_cols(grads, lax.all_gather(output_basis, "dp", axis=1, tiled=True))
    rot_in = lax.psum(part_in, "basis").astype(jnp.bfloat16)
    data_count = lax.axis_size("dp")
    panel_count = lax.axis_size("basis")
    block = K // (data_count * panel_count)
    ordered = part_out.reshape(tokens, data_count, panel_count, block)
    ordered = jnp.transpose(ordered, (0, 2, 1, 3)).reshape(tokens, K)
    rot_out = lax.psum_scatter(ordered, "basis", scatter_dimension=1, tiled=True).astype(
        jnp.bfloat16
    )
    coeff = lax.dot_general(
        rot_out, rot_in, (((0,), (0,)), ((), ())), preferred_element_type=jnp.float32
    )
    coeff = coeff / jnp.sqrt(jnp.float32(TOK))
    summed = lax.psum_scatter(coeff * coeff, "dp", scatter_dimension=0, tiled=True)
    return summed / jnp.float32(data_count)


def nt_dot(left, right):
    return lax.dot_general(
        left, right, (((1,), (1,)), ((), ())), preferred_element_type=jnp.float32
    )


def pick_kernel(outer_ref, inner_ref, out_ref):
    z = lax.axis_index("dp") // 2
    outer = (z == 0) | (z == 3)

    @pl.when(outer)
    def _():
        out_ref[...] = outer_ref[...]

    @pl.when(jnp.logical_not(outer))
    def _():
        out_ref[...] = inner_ref[...]


def cut_kernel(in_half, first, in_ref, out_ref, m0, m1, t0, t1):
    x = lax.axis_index("group")
    out_half = first + m1.shape[1]
    for side, unit0, unit1 in ((x, m0, m1), (1 - x, t0, t1)):
        in_at = pl.multiple_of(side * in_half, LANES)
        out_at = pl.multiple_of(side * out_half, LANES)
        next_at = pl.multiple_of(side * out_half + first, LANES)
        unit0[:, :in_half] = in_ref[:, pl.ds(in_at, in_half)]
        unit0[:, in_half:] = out_ref[:, pl.ds(out_at, first)]
        unit1[...] = out_ref[:, pl.ds(next_at, unit1.shape[1])]


def rotate_kernel(plan, in_half, first, acts_ref, grads_ref, *refs):
    x = lax.axis_index("group")
    core = lax.axis_index("basis")
    terms, has_acc, last = plan
    refs = list(refs)
    stack = refs.pop()
    z = lax.axis_index("dp") // 2
    outer = (z == 0) | (z == 3)
    out_half = grads_ref.shape[1] // 2
    rot_in = rot_out = None
    for mine, index, pieces in terms:
        rows = refs[0].shape[0]
        for i, (at_outer, at_inner) in enumerate(pieces):
            at = slice(i * rows, (i + 1) * rows)
            if at_outer == at_inner:
                stack[at] = refs[at_outer][...]
                continue

            @pl.when(outer)
            def _():
                stack[at] = refs[at_outer][...]

            @pl.when(jnp.logical_not(outer))
            def _():
                stack[at] = refs[at_inner][...]

        side = x if mine else 1 - x
        if index == 0:
            cols = pl.ds(pl.multiple_of(side * in_half, LANES), in_half)
            part = nt_dot(stack[:, :in_half], acts_ref[:, cols])
            rot_in = part if rot_in is None else rot_in + part
            cols = pl.ds(pl.multiple_of(side * out_half, LANES), first)
            part = nt_dot(stack[:, in_half:], grads_ref[:, cols])
        else:
            cols = pl.ds(pl.multiple_of(side * out_half + first, LANES), out_half - first)
            part = nt_dot(stack[...], grads_ref[:, cols])
        rot_out = part if rot_out is None else rot_out + part
    panel = refs[0].shape[0] // 2
    refs = refs[1 + max(i for term in terms for pair in term[2] for i in pair) :]
    if has_acc:
        if rot_in is not None:
            rot_in += refs.pop(0)[...]
        rot_out += refs.pop(0)[...]
    if rot_in is not None:
        refs.pop(0)[...] = rot_in
    if not last:
        refs.pop(0)[...] = rot_out
        return
    keep, send = refs
    for shard in range(rot_out.shape[0] // (2 * panel)):
        low = rot_out[2 * shard * panel : (2 * shard + 1) * panel]
        high = rot_out[(2 * shard + 1) * panel : 2 * (shard + 1) * panel]
        at = slice(shard * panel, (shard + 1) * panel)
        keep[at] = jnp.where(core == 0, low, high)
        send[at] = jnp.where(core == 0, high, low)


def finish_kernel(rows, *refs):
    me = lax.axis_index("dp")
    z, y = me // 2, me % 2
    order = [z]
    for by_z in ((1, 2, 1, 2), (2, 0, 3, 1), (3, 3, 0, 0)):
        order.append(jnp.where(z == 0, by_z[0], jnp.where(z == 1, by_z[1], jnp.where(z == 2, by_z[2], by_z[3]))))
    ins, keep, come = refs[0:4], refs[4:6], refs[6:8]
    outs = refs[8:-2]
    in_ref, out_ref = refs[-2:]
    half = rows // 2
    for shard in range(8):
        part, local = (0, shard) if shard < 2 else (1, shard - 2)
        owner = order[shard // 2] * 2 + (y if shard % 2 == 0 else 1 - y)
        block = ins[2 * part][pl.ds(local * rows, rows)] + ins[2 * part + 1][pl.ds(local * rows, rows)]
        in_ref[pl.ds(pl.multiple_of(owner * rows, 16), rows), :] = block.astype(jnp.bfloat16)
        place = owner ^ me
        at = pl.ds(local * half, half)
        out_ref[pl.ds(pl.multiple_of(place * half, 8), half), :] = keep[part][at] + come[part][at]
    coeff = nt_dot(out_ref[...].astype(jnp.bfloat16), in_ref[...])
    coeff = coeff * (1.0 / TOK**0.5)
    square = coeff * coeff
    for place, ref in enumerate(outs):
        ref[...] = square[place * half : (place + 1) * half]


def per_device_plane(activations, out_grads, input_basis, output_basis):
    acts, grads = activations[0], out_grads[0]
    in_t, out_t = input_basis.T, output_basis.T
    rows = in_t.shape[0]
    tokens = acts.shape[0]
    me = lax.axis_index("dp")
    z, y = me // 2, me % 2
    in_half = in_t.shape[1] // 2
    width = (in_t.shape[1] + out_t.shape[1]) // 4
    first = width - in_half

    vmem = pl.BlockSpec(memory_space=pltpu.VMEM)

    def swap_core(value):
        return lax.ppermute(value, "basis", [(0, 1), (1, 0)])

    unit = jax.ShapeDtypeStruct((rows, width), in_t.dtype)
    m0, m1, t0, t1 = pl.pallas_call(
        functools.partial(cut_kernel, in_half, first),
        out_shape=[unit] * 4,
        in_specs=[vmem] * 2,
        out_specs=[vmem] * 4,
        compiler_params=pltpu.CompilerParams(vmem_limit_bytes=8 * 2**20),
        name="cut",
    )(in_t, out_t)

    def rotate(slots, names, acc, last):
        terms, pieces, out_shape = [], [], []
        count = 2 * len(slots)

        def ref_of(value):
            for i, piece in enumerate(pieces):
                if piece is value:
                    return i
            pieces.append(value)
            return len(pieces) - 1

        for name in names:
            terms.append((name[0] == "m", int(name[1]), [
                (ref_of(at_outer[s + k]), ref_of(at_inner[s + k])) for s in slots for k in (name, "o" + name)
            ]))
        full = jax.ShapeDtypeStruct((count * rows, tokens), jnp.float32)
        panel = jax.ShapeDtypeStruct((count * rows // 2, tokens), jnp.float32)
        if any(name[1] == "0" for name in names):
            out_shape.append(full)
        out_shape += [panel, panel] if last else [full]
        return pl.pallas_call(
            functools.partial(rotate_kernel, (terms, bool(acc), last), in_half, first),
            out_shape=out_shape,
            in_specs=[vmem] * (2 + len(pieces) + len(acc)),
            out_specs=[vmem] * len(out_shape),
            scratch_shapes=[pltpu.VMEM((count * rows, width), in_t.dtype)],
            compiler_params=pltpu.CompilerParams(vmem_limit_bytes=20 * 2**20),
            cost_estimate=pl.CostEstimate(
                flops=2 * len(names) * count * rows * width * tokens,
                bytes_accessed=2 * len(pieces) * rows * width,
                transcendentals=0,
            ),
            name="rotate",
        )(acts, grads, *pieces, *acc)

    outer = (z == 0) | (z == 3)
    cells = range(8)
    link_a = [(i, i ^ 2) for i in cells]
    link_b = [(i, 2 * (3 - i // 2) + i % 2) for i in cells if 2 <= i < 6]
    link_y = [(i, i ^ 1) for i in cells]
    at_ends = [i for i in cells if i < 2 or i >= 6]

    def group_pairs(pairs):
        return [(8 * g + a, 8 * g + b) for g in range(2) for a, b in pairs]

    def across_x(where):
        return [(8 * g + i, 8 * (1 - g) + i) for g in range(2) for i in where]

    def send(value, pairs):
        return lax.ppermute(value, ("group", "dp"), pairs)

    def pick(for_outer, for_inner):
        if for_outer is for_inner:
            return for_outer
        return pl.pallas_call(
            pick_kernel,
            out_shape=unit,
            in_specs=[vmem] * 2,
            out_specs=vmem,
            compiler_params=pltpu.CompilerParams(vmem_limit_bytes=4 * 2**20),
            cost_estimate=pl.CostEstimate(flops=STEP, bytes_accessed=8192, transcendentals=0),
            name="pick",
        )(for_outer, for_inner)

    at_outer = {"0m0": m0, "0m1": m1, "0t0": t0, "0t1": t1}
    at_inner = dict(at_outer)
    a_outer = ["1m0", "1m1", "2m0", "2m1", "3m0", "3m1", "3om0", "3t0", "3ot0", "3t1"]
    a_inner = ["2m0", "2m1", "2om0", "2t0", "2ot0", "2t1", "2om1", "2ot1"]
    b_inner = ["1m0", "1m1", "3m0", "3m1", "3om0", "3t0", "3ot0", "3t1", "3om1", "3ot1"]
    y_outer = ["0om0", "0om1", "1om0", "1om1", "2om0", "2om1", "1ot1", "3om1", "2ot0", "2ot1"]
    x_outer = [None, None, "0ot0", "0ot1", "1t1", "2t0", "1t0", "2t1", "1ot0", "3ot1"]
    y_inner = ["0om0", "0om1", None, None, "1om0", "1om1", None, None, None, "1ot1"]
    x_inner = [None, None, "0ot0", "0ot1", None, None, "1t0", "1t1", "1ot0", None]
    to_inner = ["0" + name[1:] for name in a_inner]

    def over_y(name):
        return name.replace("o", "")

    def over_x(name):
        return name.translate(str.maketrans("mt", "tm"))

    extra, sent = {}, []

    def settle():
        if len(sent) >= AHEAD:
            extra["sent"] = sent[-AHEAD]
        spots = [(u, k) for u in (at_outer, at_inner, extra) for k in u]
        unique = {id(u[k]): u[k] for u, k in spots}
        fresh = dict(zip(unique, lax.optimization_barrier(tuple(unique.values()))))
        for u, k in spots:
            u[k] = fresh[id(u[k])]

    def bring(value, pairs, *landings):
        got = send(value, pairs)
        sent.append(got)
        return [(units, name, got) for units, name in landings]

    landing = {}
    for r in range(1, 11):
        i = r - 1
        for units, name, value in landing.pop(r - 2, []):
            units[name] = value
        settle()
        outward = at_inner["0" + a_outer[i][1:]] if r < 3 else at_inner[b_inner[i - 2]]
        if r < 9:
            value, pairs = pick(at_outer[to_inner[i]], outward), group_pairs(link_a)
            spots = [(at_outer, a_outer[i]), (at_inner, a_inner[i])]
        else:
            value, pairs = outward, group_pairs([p for p in link_a if p[1] in at_ends])
            spots = [(at_outer, a_outer[i])]
        landing[r] = bring(value, pairs, *spots)
        settle()
        crossing = at_inner["0" + b_inner[i][1:]] if r < 3 else at_inner[a_inner[i - 2]]
        value = at_outer[over_y(y_outer[i])]
        spots = [(at_outer, y_outer[i])]
        if y_inner[i]:
            value, pairs = pick(value, at_inner[over_y(y_inner[i])]), group_pairs(link_y)
            spots.append((at_inner, y_inner[i]))
        else:
            y_pairs = [p for p in link_y if p[0] in at_ends]
            value, pairs = pick(value, crossing), group_pairs(y_pairs + link_b)
            spots.append((at_inner, b_inner[i]))
        landing[r] += bring(value, pairs, *spots)
        settle()
        if x_inner[i]:
            value = pick(at_outer[over_x(x_outer[i])], at_inner[over_x(x_inner[i])])
            spots, pairs = [(at_inner, x_inner[i])], across_x(cells)
        else:
            crossing = at_inner["0" + b_inner[i][1:]] if r < 3 else at_inner[a_inner[i - 2]]
            spots, pairs = [(at_inner, b_inner[i])], group_pairs(link_b)
            value = crossing
            if x_outer[i]:
                value = pick(at_outer[over_x(x_outer[i])], crossing)
                pairs = across_x(at_ends) + pairs
        if x_outer[i]:
            spots.append((at_outer, x_outer[i]))
        landing[r] += bring(value, pairs, *spots)
        if r == 7:
            extra["in_a"], extra["keep_a"], extra["send_a"] = rotate("0", ["m0", "m1", "t0", "t1"], [], True)
        if r == 9:
            extra["acc_in"], extra["acc_out"] = rotate("123", ["m0"], [], False)
    for r in (9, 10):
        for units, name, value in landing.pop(r):
            units[name] = value
    in_a, keep_a, send_a = extra["in_a"], extra["keep_a"], extra["send_a"]
    in_b, acc_out = rotate("123", ["t0"], [extra["acc_in"], extra["acc_out"]], False)
    (acc_out,) = rotate("123", ["m1"], [acc_out], False)
    keep_b, send_b = rotate("123", ["t1"], [acc_out], True)

    squares = pl.pallas_call(
        functools.partial(finish_kernel, rows),
        out_shape=[jax.ShapeDtypeStruct((rows // 2, K), jnp.float32)] * 8,
        in_specs=[vmem] * 8,
        out_specs=[vmem] * 8,
        scratch_shapes=[
            pltpu.VMEM((K, tokens), jnp.bfloat16),
            pltpu.VMEM((K // 2, tokens), jnp.float32),
        ],
        compiler_params=pltpu.CompilerParams(vmem_limit_bytes=8 * 2**20),
        name="finish",
    )(
        in_a, swap_core(in_a), in_b, swap_core(in_b),
        keep_a, keep_b, swap_core(send_a), swap_core(send_b),
    )
    total = squares[0]
    for k in range(1, 8):
        total = total + lax.ppermute(squares[k], "dp", [(i, i ^ k) for i in range(8)])
    return total * (1.0 / 8)


def solution(mesh):
    in_specs = (
        P(("group", "dp"), None, "basis"),
        P(("group", "dp"), None, "basis"),
        P("basis", "dp"),
        P("basis", "dp"),
    )
    out_specs = P(("group", "dp", "basis"), None)
    plane = (mesh.shape["group"], mesh.shape["dp"], mesh.shape["basis"]) == (2, 8, 2)
    return jax.shard_map(
        per_device_plane if plane else per_device_any,
        mesh=mesh,
        in_specs=in_specs,
        out_specs=out_specs,
        check_vma=False,
    )
```

```python
import functools

import jax
import jax.numpy as jnp
from jax import lax
from jax.experimental import pallas as pl
from jax.experimental.pallas import tpu as pltpu
from jax.sharding import PartitionSpec as P

TOK = 256
K = 384
LANES = 128
AHEAD = 30
ORDER = "APQ"
STEP = 1 * 10**8


def place_cols(left, piece):
    product = jnp.dot(left, piece, preferred_element_type=jnp.float32)
    return product


def per_device_any(activations, out_grads, input_basis, output_basis):
    acts = activations[0]
    grads = out_grads[0]
    tokens = acts.shape[0]
    part_in = place_cols(acts, lax.all_gather(input_basis, "dp", axis=1, tiled=True))
    part_out = place_cols(grads, lax.all_gather(output_basis, "dp", axis=1, tiled=True))
    rot_in = lax.psum(part_in, "basis").astype(jnp.bfloat16)
    data_count = lax.axis_size("dp")
    panel_count = lax.axis_size("basis")
    block = K // (data_count * panel_count)
    ordered = part_out.reshape(tokens, data_count, panel_count, block)
    ordered = jnp.transpose(ordered, (0, 2, 1, 3)).reshape(tokens, K)
    rot_out = lax.psum_scatter(ordered, "basis", scatter_dimension=1, tiled=True).astype(
        jnp.bfloat16
    )
    coeff = lax.dot_general(
        rot_out, rot_in, (((0,), (0,)), ((), ())), preferred_element_type=jnp.float32
    )
    coeff = coeff / jnp.sqrt(jnp.float32(TOK))
    summed = lax.psum_scatter(coeff * coeff, "dp", scatter_dimension=0, tiled=True)
    return summed / jnp.float32(data_count)


def nt_dot(left, right):
    return lax.dot_general(
        left, right, (((1,), (1,)), ((), ())), preferred_element_type=jnp.float32
    )


def pick_kernel(outer_ref, inner_ref, out_ref):
    z = lax.axis_index("dp") // 2
    outer = (z == 0) | (z == 3)

    @pl.when(outer)
    def _():
        out_ref[...] = outer_ref[...]

    @pl.when(jnp.logical_not(outer))
    def _():
        out_ref[...] = inner_ref[...]


def cut_kernel(in_half, first, in_ref, out_ref, m0, m1, t0, t1, sems):
    x = lax.axis_index("group")
    out_half = first + m1.shape[1]
    copies = []
    for side, unit0, unit1 in ((x, m0, m1), (1 - x, t0, t1)):
        in_at = pl.multiple_of(side * in_half, LANES)
        out_at = pl.multiple_of(side * out_half, LANES)
        next_at = pl.multiple_of(side * out_half + first, LANES)
        copies += [
            (in_ref.at[:, pl.ds(in_at, in_half)], unit0.at[:, :in_half]),
            (out_ref.at[:, pl.ds(out_at, first)], unit0.at[:, in_half:]),
            (out_ref.at[:, pl.ds(next_at, unit1.shape[1])], unit1),
        ]
    started = [pltpu.make_async_copy(a, b, sems.at[i]) for i, (a, b) in enumerate(copies)]
    for copy in started:
        copy.start()
    for copy in started:
        copy.wait()


def rotate_kernel(plan, in_half, first, acts_ref, grads_ref, *refs):
    x = lax.axis_index("group")
    core = lax.axis_index("basis")
    terms, acc_from, last = plan
    refs = list(refs)
    stack = refs.pop()
    z = lax.axis_index("dp") // 2
    outer = (z == 0) | (z == 3)
    out_half = grads_ref.shape[1] // 2
    rot_in = rot_out = None
    for mine, index, pieces in terms:
        rows = refs[0].shape[0]
        for i, (at_outer, at_inner) in enumerate(pieces):
            at = slice(i * rows, (i + 1) * rows)
            if at_outer == at_inner:
                stack[at] = refs[at_outer][...]
                continue

            @pl.when(outer)
            def _():
                stack[at] = refs[at_outer][...]

            @pl.when(jnp.logical_not(outer))
            def _():
                stack[at] = refs[at_inner][...]

        side = x if mine else 1 - x
        if index == 0:
            cols = pl.ds(pl.multiple_of(side * in_half, LANES), in_half)
            part = nt_dot(stack[:, :in_half], acts_ref[:, cols])
            rot_in = part if rot_in is None else rot_in + part
            cols = pl.ds(pl.multiple_of(side * out_half, LANES), first)
            part = nt_dot(stack[:, in_half:], grads_ref[:, cols])
        else:
            cols = pl.ds(pl.multiple_of(side * out_half + first, LANES), out_half - first)
            part = nt_dot(stack[...], grads_ref[:, cols])
        rot_out = part if rot_out is None else rot_out + part
    panel = refs[0].shape[0] // 2
    refs = refs[1 + max(i for term in terms for pair in term[2] for i in pair) :]
    if acc_from is not None:
        at = slice(acc_from, acc_from + rot_out.shape[0])
        if rot_in is not None:
            rot_in += refs.pop(0)[at]
        rot_out += refs.pop(0)[at]
    if rot_in is not None:
        refs.pop(0)[...] = rot_in
    if not last:
        refs.pop(0)[...] = rot_out
        return
    keep, send = refs
    for shard in range(rot_out.shape[0] // (2 * panel)):
        low = rot_out[2 * shard * panel : (2 * shard + 1) * panel]
        high = rot_out[(2 * shard + 1) * panel : 2 * (shard + 1) * panel]
        at = slice(shard * panel, (shard + 1) * panel)
        keep[at] = jnp.where(core == 0, low, high)
        send[at] = jnp.where(core == 0, high, low)


def store_squares(keep, come, rot_in, outs):
    rot_out = (keep[...] + come[...]).astype(jnp.bfloat16)
    coeff = nt_dot(rot_out, rot_in) * (1.0 / TOK**0.5)
    square = coeff * coeff
    panel = outs[0].shape[0]
    for block, ref in enumerate(outs):
        ref[...] = square[block * panel : (block + 1) * panel]


def rotated_kernel(rows, in_a, in_a2, in_b, in_b2, keep, come, in_ref, *outs):
    me = lax.axis_index("dp")
    for block in range(8):
        at = pl.ds((block if block < 2 else block - 2) * rows, rows)
        total = in_a[at] + in_a2[at] if block < 2 else in_b[at] + in_b2[at]
        begin = pl.multiple_of((me ^ block) * rows, 16)
        in_ref[pl.ds(begin, rows), :] = total.astype(jnp.bfloat16)
    store_squares(keep, come, in_ref[...], outs)


def squares_kernel(in_ref, keep, come, *outs):
    store_squares(keep, come, in_ref[...], outs)


def per_device_plane(activations, out_grads, input_basis, output_basis):
    acts, grads = activations[0], out_grads[0]
    in_t, out_t = input_basis.T, output_basis.T
    rows = in_t.shape[0]
    tokens = acts.shape[0]
    me = lax.axis_index("dp")
    z, y = me // 2, me % 2
    in_half = in_t.shape[1] // 2
    width = (in_t.shape[1] + out_t.shape[1]) // 4
    first = width - in_half

    vmem = pl.BlockSpec(memory_space=pltpu.VMEM)

    def swap_core(value):
        return lax.ppermute(value, "basis", [(0, 1), (1, 0)])

    unit = jax.ShapeDtypeStruct((rows, width), in_t.dtype)
    m0, m1, t0, t1 = pl.pallas_call(
        functools.partial(cut_kernel, in_half, first),
        out_shape=[unit] * 4,
        in_specs=[pl.BlockSpec(memory_space=pltpu.HBM)] * 2,
        out_specs=[vmem] * 4,
        scratch_shapes=[pltpu.SemaphoreType.DMA((6,))],
        compiler_params=pltpu.CompilerParams(vmem_limit_bytes=8 * 2**20),
        name="cut",
    )(in_t, out_t)

    def rotate(slots, names, acc, acc_from, last):
        terms, pieces, out_shape = [], [], []
        count = 2 * len(slots)

        def ref_of(value):
            for i, piece in enumerate(pieces):
                if piece is value:
                    return i
            pieces.append(value)
            return len(pieces) - 1

        for name in names:
            terms.append((name[0] == "m", int(name[1]), [
                (ref_of(at_outer[s + k]), ref_of(at_inner[s + k])) for s in slots for k in (name, "o" + name)
            ]))
        full = jax.ShapeDtypeStruct((count * rows, tokens), jnp.float32)
        panel = jax.ShapeDtypeStruct((count * rows // 2, tokens), jnp.float32)
        if any(name[1] == "0" for name in names):
            out_shape.append(full)
        out_shape += [panel, panel] if last else [full]
        return pl.pallas_call(
            functools.partial(rotate_kernel, (terms, acc_from, last), in_half, first),
            out_shape=out_shape,
            in_specs=[vmem] * (2 + len(pieces) + len(acc)),
            out_specs=[vmem] * len(out_shape),
            scratch_shapes=[pltpu.VMEM((count * rows, width), in_t.dtype)],
            compiler_params=pltpu.CompilerParams(vmem_limit_bytes=20 * 2**20),
            cost_estimate=pl.CostEstimate(
                flops=2 * len(names) * count * rows * width * tokens,
                bytes_accessed=2 * len(pieces) * rows * width,
                transcendentals=0,
            ),
            name="rotate",
        )(acts, grads, *pieces, *acc)

    outer = (z == 0) | (z == 3)
    cells = range(8)
    link_a = [(i, i ^ 2) for i in cells]
    link_b = [(i, 2 * (3 - i // 2) + i % 2) for i in cells if 2 <= i < 6]
    link_y = [(i, i ^ 1) for i in cells]
    at_ends = [i for i in cells if i < 2 or i >= 6]

    def group_pairs(pairs):
        return [(8 * g + a, 8 * g + b) for g in range(2) for a, b in pairs]

    def across_x(where):
        return [(8 * g + i, 8 * (1 - g) + i) for g in range(2) for i in where]

    def send(value, pairs):
        return lax.ppermute(value, ("group", "dp"), pairs)

    def pick(for_outer, for_inner):
        if for_outer is for_inner:
            return for_outer
        return pl.pallas_call(
            pick_kernel,
            out_shape=unit,
            in_specs=[vmem] * 2,
            out_specs=vmem,
            compiler_params=pltpu.CompilerParams(vmem_limit_bytes=4 * 2**20),
            cost_estimate=pl.CostEstimate(flops=STEP, bytes_accessed=8192, transcendentals=0),
            name="pick",
        )(for_outer, for_inner)

    at_outer = {"0m0": m0, "0m1": m1, "0t0": t0, "0t1": t1}
    at_inner = dict(at_outer)
    a_outer = ["1m0", "1m1", "2m0", "2m1", "3m0", "3t0", "3m1", "3om0", "3ot1", "1ot1"]
    outward = ["0m0", "0m1", "3m0", "3m1", "2m0", "2t0", "2m1", "2om0", "2ot1", "0ot1"]
    a_inner = ["1m0", "1t0", "1m1", "1om0", "1ot1", "1ot0", "1t1", "3om1", "3t1", "1om1"]
    inward = ["0m0", "0t0", "0m1", "0om0", "0ot1", "0ot0", "0t1", "2om1", "2t1", "0om1"]
    b_inner = ["3m0", "3m1", "2m0", "2t0", "2m1", "2om0", "2ot1", "2ot0", "3ot1", None]
    crossing = ["0m0", "0m1", "1m0", "1t0", "1m1", "1om0", "1ot1", "1ot0", "0ot1", None]
    y_outer = ["0om1", "0om0", "1om0", "0ot0", "2om0", "2om1", "2ot0", "3ot0", "3om1", "1om1"]
    x_outer = [None, None, "0ot1", "1t0", "2t0", "2t1", "1ot0", "2ot1", "3t1", "1t1"]
    y_inner = ["0om1", "0om0", None, "0ot0", "3om0", None, None, "2om1", None, None]
    x_inner = [None, None, "0ot1", None, None, "3t0", "3ot0", None, "2t1", None]

    def over_y(name):
        return name.replace("o", "")

    def over_x(name):
        return name.translate(str.maketrans("mt", "tm"))

    extra, sent = {}, []

    def settle():
        if len(sent) >= AHEAD:
            extra["sent"] = sent[-AHEAD]
        spots = [(u, k) for u in (at_outer, at_inner, extra) for k in u]
        unique = {id(u[k]): u[k] for u, k in spots}
        fresh = dict(zip(unique, lax.optimization_barrier(tuple(unique.values()))))
        for u, k in spots:
            u[k] = fresh[id(u[k])]

    def bring(value, pairs, *landings):
        got = send(value, pairs)
        sent.append(got)
        return [(units, name, got) for units, name in landings]

    landing = {}
    for r in range(1, 11):
        i = r - 1
        for units, name, value in landing.pop(r - 2, []):
            units[name] = value
        if r == 7:
            extra["in_a"], extra["keep_a"], extra["send_a"] = rotate("0", ["m0", "m1", "t0", "t1"], [], None, True)
        landing[r] = []
        if r == 10:
            acc_in, acc_out = rotate("123", ["m0"], [], None, False)
            extra["in_b"], extra["acc"] = rotate("123", ["t0"], [acc_in, acc_out], 0, False)
        for link in ORDER if r > 2 else "APQ":
            settle()
            if link == "A":
                value = pick(at_outer[inward[i]], at_inner[outward[i]])
                landing[r] += bring(value, group_pairs(link_a), (at_outer, a_outer[i]), (at_inner, a_inner[i]))
                continue
            over, from_outer, from_inner, around = (
                (over_y, y_outer[i], y_inner[i], lambda where: group_pairs([p for p in link_y if p[0] in where]))
                if link == "P"
                else (over_x, x_outer[i], x_inner[i], across_x)
            )
            spots, pairs, choices = [], [], []
            if from_outer:
                spots.append((at_outer, from_outer))
                choices.append(at_outer[over(from_outer)])
                pairs += around(at_ends)
            if from_inner:
                spots.append((at_inner, from_inner))
                choices.append(at_inner[over(from_inner)])
                pairs += around([c for c in cells if c not in at_ends])
            elif b_inner[i]:
                spots.append((at_inner, b_inner[i]))
                choices.append(at_inner[crossing[i]])
                pairs += group_pairs(link_b)
            landing[r] += bring(pick(choices[0], choices[-1]), pairs, *spots)

    block = jax.ShapeDtypeStruct((rows // 2, K), jnp.float32)

    def squares(kernel, name, out_shape, *values):
        return pl.pallas_call(
            kernel,
            out_shape=out_shape,
            in_specs=[vmem] * len(values),
            out_specs=[vmem] * len(out_shape),
            compiler_params=pltpu.CompilerParams(vmem_limit_bytes=6 * 2**20),
            name=name,
        )(*values)

    def to_owner(k, value):
        return lax.ppermute(value, "dp", [(i, i ^ k) for i in range(8)])

    in_a, keep_a, send_a = extra["in_a"], extra["keep_a"], extra["send_a"]
    in_b, acc = extra["in_b"], extra["acc"]
    rot_in, *near = squares(
        functools.partial(rotated_kernel, rows), "rotated",
        [jax.ShapeDtypeStruct((K, tokens), jnp.bfloat16)] + [block] * 2,
        in_a, swap_core(in_a), in_b, swap_core(in_b), keep_a, swap_core(send_a),
    )
    early = near[0] + to_owner(1, near[1])
    for units, name, value in landing.pop(9):
        units[name] = value
    keep_b, send_b = rotate("23", ["m1", "t1"], [acc], 2 * rows, True)
    far = squares(squares_kernel, "squares", [block] * 4, rot_in, keep_b, swap_core(send_b))
    for k in range(4):
        early = early + to_owner(4 + k, far[k])

    for units, name, value in landing.pop(10):
        units[name] = value
    keep_c, send_c = rotate("1", ["m1", "t1"], [acc], 0, True)
    early, come_c = lax.optimization_barrier((early, swap_core(send_c)))
    late = squares(squares_kernel, "squares", [block] * 2, rot_in, keep_c, come_c)
    total = early + to_owner(2, late[0]) + to_owner(3, late[1])
    return total * (1.0 / 8)


def solution(mesh):
    in_specs = (
        P(("group", "dp"), None, "basis"),
        P(("group", "dp"), None, "basis"),
        P("basis", "dp"),
        P("basis", "dp"),
    )
    out_specs = P(("group", "dp", "basis"), None)
    plane = (mesh.shape["group"], mesh.shape["dp"], mesh.shape["basis"]) == (2, 8, 2)
    return jax.shard_map(
        per_device_plane if plane else per_device_any,
        mesh=mesh,
        in_specs=in_specs,
        out_specs=out_specs,
        check_vma=False,
    )
```

```python
import functools

import jax
import jax.numpy as jnp
from jax import lax
from jax.experimental import pallas as pl
from jax.experimental.pallas import tpu as pltpu
from jax.sharding import PartitionSpec as P

TOK = 256
K = 384
LANES = 128
AHEAD = 30
ORDER = "APQ"
STEP = 5 * 10**8


def place_cols(left, piece):
    product = jnp.dot(left, piece, preferred_element_type=jnp.float32)
    return product


def per_device_any(activations, out_grads, input_basis, output_basis):
    acts = activations[0]
    grads = out_grads[0]
    tokens = acts.shape[0]
    part_in = place_cols(acts, lax.all_gather(input_basis, "dp", axis=1, tiled=True))
    part_out = place_cols(grads, lax.all_gather(output_basis, "dp", axis=1, tiled=True))
    rot_in = lax.psum(part_in, "basis").astype(jnp.bfloat16)
    data_count = lax.axis_size("dp")
    panel_count = lax.axis_size("basis")
    block = K // (data_count * panel_count)
    ordered = part_out.reshape(tokens, data_count, panel_count, block)
    ordered = jnp.transpose(ordered, (0, 2, 1, 3)).reshape(tokens, K)
    rot_out = lax.psum_scatter(ordered, "basis", scatter_dimension=1, tiled=True).astype(
        jnp.bfloat16
    )
    coeff = lax.dot_general(
        rot_out, rot_in, (((0,), (0,)), ((), ())), preferred_element_type=jnp.float32
    )
    coeff = coeff / jnp.sqrt(jnp.float32(TOK))
    summed = lax.psum_scatter(coeff * coeff, "dp", scatter_dimension=0, tiled=True)
    return summed / jnp.float32(data_count)


def nt_dot(left, right):
    return lax.dot_general(
        left, right, (((1,), (1,)), ((), ())), preferred_element_type=jnp.float32
    )


def pick_kernel(outer_ref, inner_ref, out_ref):
    z = lax.axis_index("dp") // 2
    outer = (z == 0) | (z == 3)

    @pl.when(outer)
    def _():
        out_ref[...] = outer_ref[...]

    @pl.when(jnp.logical_not(outer))
    def _():
        out_ref[...] = inner_ref[...]


def first_cut_kernel(in_ref, out_ref, m0, sems):
    x = lax.axis_index("group")
    in_half = in_ref.shape[1] // 2
    first = m0.shape[1] - in_half
    in_at = pl.multiple_of(x * in_half, LANES)
    out_at = pl.multiple_of(x * (out_ref.shape[1] // 2), LANES)
    ins = pltpu.make_async_copy(in_ref.at[:, pl.ds(in_at, in_half)], m0.at[:, :in_half], sems.at[0])
    outs = pltpu.make_async_copy(out_ref.at[:, pl.ds(out_at, first)], m0.at[:, in_half:], sems.at[1])
    ins.start()
    outs.start()
    ins.wait()
    outs.wait()


def cut_kernel(in_half, first, in_ref, out_ref, m1, t0, t1):
    x = lax.axis_index("group")
    out_half = first + m1.shape[1]
    for side, unit0, unit1 in ((x, None, m1), (1 - x, t0, t1)):
        in_at = pl.multiple_of(side * in_half, LANES)
        out_at = pl.multiple_of(side * out_half, LANES)
        next_at = pl.multiple_of(side * out_half + first, LANES)
        if unit0 is not None:
            unit0[:, :in_half] = in_ref[:, pl.ds(in_at, in_half)]
            unit0[:, in_half:] = out_ref[:, pl.ds(out_at, first)]
        unit1[...] = out_ref[:, pl.ds(next_at, unit1.shape[1])]


def rotate_kernel(plan, in_half, first, acts_ref, grads_ref, *refs):
    x = lax.axis_index("group")
    core = lax.axis_index("basis")
    terms, acc_from, last = plan
    refs = list(refs)
    stack = refs.pop()
    z = lax.axis_index("dp") // 2
    outer = (z == 0) | (z == 3)
    out_half = grads_ref.shape[1] // 2
    rot_in = rot_out = None
    for mine, index, pieces in terms:
        rows = refs[0].shape[0]
        for i, (at_outer, at_inner) in enumerate(pieces):
            at = slice(i * rows, (i + 1) * rows)
            if at_outer == at_inner:
                stack[at] = refs[at_outer][...]
                continue

            @pl.when(outer)
            def _():
                stack[at] = refs[at_outer][...]

            @pl.when(jnp.logical_not(outer))
            def _():
                stack[at] = refs[at_inner][...]

        side = x if mine else 1 - x
        if index == 0:
            cols = pl.ds(pl.multiple_of(side * in_half, LANES), in_half)
            part = nt_dot(stack[:, :in_half], acts_ref[:, cols])
            rot_in = part if rot_in is None else rot_in + part
            cols = pl.ds(pl.multiple_of(side * out_half, LANES), first)
            part = nt_dot(stack[:, in_half:], grads_ref[:, cols])
        else:
            cols = pl.ds(pl.multiple_of(side * out_half + first, LANES), out_half - first)
            part = nt_dot(stack[...], grads_ref[:, cols])
        rot_out = part if rot_out is None else rot_out + part
    panel = refs[0].shape[0] // 2
    refs = refs[1 + max(i for term in terms for pair in term[2] for i in pair) :]
    if acc_from is not None:
        at = slice(acc_from, acc_from + rot_out.shape[0])
        if rot_in is not None:
            rot_in += refs.pop(0)[at]
        rot_out += refs.pop(0)[at]
    if rot_in is not None:
        refs.pop(0)[...] = rot_in
    if not last:
        refs.pop(0)[...] = rot_out
        return
    keep, send = refs
    for shard in range(rot_out.shape[0] // (2 * panel)):
        low = rot_out[2 * shard * panel : (2 * shard + 1) * panel]
        high = rot_out[(2 * shard + 1) * panel : 2 * (shard + 1) * panel]
        at = slice(shard * panel, (shard + 1) * panel)
        keep[at] = jnp.where(core == 0, low, high)
        send[at] = jnp.where(core == 0, high, low)


def store_squares(keep, come, rot_in, outs):
    rot_out = (keep[...] + come[...]).astype(jnp.bfloat16)
    coeff = nt_dot(rot_out, rot_in) * (1.0 / TOK**0.5)
    square = coeff * coeff
    panel = outs[0].shape[0]
    for block, ref in enumerate(outs):
        ref[...] = square[block * panel : (block + 1) * panel].astype(ref.dtype)


def rotated_kernel(rows, in_a, in_a2, in_b, in_b2, keep, come, in_ref, *outs):
    me = lax.axis_index("dp")
    for block in range(8):
        at = pl.ds((block if block < 2 else block - 2) * rows, rows)
        total = in_a[at] + in_a2[at] if block < 2 else in_b[at] + in_b2[at]
        begin = pl.multiple_of((me ^ block) * rows, 16)
        in_ref[pl.ds(begin, rows), :] = total.astype(jnp.bfloat16)
    store_squares(keep, come, in_ref[...], outs)


def squares_kernel(in_ref, keep, come, *outs):
    store_squares(keep, come, in_ref[...], outs)


def per_device_plane(activations, out_grads, input_basis, output_basis):
    acts, grads = activations[0], out_grads[0]
    in_t, out_t = input_basis.T, output_basis.T
    rows = in_t.shape[0]
    tokens = acts.shape[0]
    me = lax.axis_index("dp")
    z, y = me // 2, me % 2
    in_half = in_t.shape[1] // 2
    width = (in_t.shape[1] + out_t.shape[1]) // 4
    first = width - in_half

    vmem = pl.BlockSpec(memory_space=pltpu.VMEM)

    def swap_core(value):
        return lax.ppermute(value, "basis", [(0, 1), (1, 0)])

    unit = jax.ShapeDtypeStruct((rows, width), in_t.dtype)
    m0 = pl.pallas_call(
        first_cut_kernel,
        out_shape=unit,
        in_specs=[pl.BlockSpec(memory_space=pltpu.HBM)] * 2,
        out_specs=vmem,
        scratch_shapes=[pltpu.SemaphoreType.DMA((2,))],
        compiler_params=pltpu.CompilerParams(vmem_limit_bytes=62 * 2**20),
        name="first_cut",
    )(in_t, out_t)
    m1, t0, t1 = pl.pallas_call(
        functools.partial(cut_kernel, in_half, first),
        out_shape=[unit] * 3,
        in_specs=[vmem] * 2,
        out_specs=[vmem] * 3,
        compiler_params=pltpu.CompilerParams(vmem_limit_bytes=8 * 2**20),
        name="cut",
    )(in_t, out_t)

    def rotate(slots, names, acc, acc_from, last):
        terms, pieces, out_shape = [], [], []
        count = 2 * len(slots)

        def ref_of(value):
            for i, piece in enumerate(pieces):
                if piece is value:
                    return i
            pieces.append(value)
            return len(pieces) - 1

        for name in names:
            terms.append((name[0] == "m", int(name[1]), [
                (ref_of(at_outer[s + k]), ref_of(at_inner[s + k])) for s in slots for k in (name, "o" + name)
            ]))
        full = jax.ShapeDtypeStruct((count * rows, tokens), jnp.float32)
        panel = jax.ShapeDtypeStruct((count * rows // 2, tokens), jnp.float32)
        if any(name[1] == "0" for name in names):
            out_shape.append(full)
        out_shape += [panel, panel] if last else [full]
        return pl.pallas_call(
            functools.partial(rotate_kernel, (terms, acc_from, last), in_half, first),
            out_shape=out_shape,
            in_specs=[vmem] * (2 + len(pieces) + len(acc)),
            out_specs=[vmem] * len(out_shape),
            scratch_shapes=[pltpu.VMEM((count * rows, width), in_t.dtype)],
            compiler_params=pltpu.CompilerParams(vmem_limit_bytes=20 * 2**20),
            cost_estimate=pl.CostEstimate(
                flops=2 * len(names) * count * rows * width * tokens,
                bytes_accessed=2 * len(pieces) * rows * width,
                transcendentals=0,
            ),
            name="rotate",
        )(acts, grads, *pieces, *acc)

    outer = (z == 0) | (z == 3)
    cells = range(8)
    link_a = [(i, i ^ 2) for i in cells]
    link_b = [(i, 2 * (3 - i // 2) + i % 2) for i in cells if 2 <= i < 6]
    link_y = [(i, i ^ 1) for i in cells]
    at_ends = [i for i in cells if i < 2 or i >= 6]

    def group_pairs(pairs):
        return [(8 * g + a, 8 * g + b) for g in range(2) for a, b in pairs]

    def across_x(where):
        return [(8 * g + i, 8 * (1 - g) + i) for g in range(2) for i in where]

    def send(value, pairs):
        return lax.ppermute(value, ("group", "dp"), pairs)

    def pick(for_outer, for_inner):
        if for_outer is for_inner:
            return for_outer
        return pl.pallas_call(
            pick_kernel,
            out_shape=unit,
            in_specs=[vmem] * 2,
            out_specs=vmem,
            compiler_params=pltpu.CompilerParams(vmem_limit_bytes=4 * 2**20),
            cost_estimate=pl.CostEstimate(flops=STEP, bytes_accessed=8192, transcendentals=0),
            name="pick",
        )(for_outer, for_inner)

    at_outer = {"0m0": m0, "0m1": m1, "0t0": t0, "0t1": t1}
    at_inner = dict(at_outer)
    a_outer = ["1m0", "1m1", "2m0", "2m1", "3m0", "3t0", "3m1", "3om0", "3ot1", "1ot1"]
    outward = ["0m0", "0m1", "3m0", "3m1", "2m0", "2t0", "2m1", "2om0", "2ot1", "0ot1"]
    a_inner = ["1m0", "1t0", "1m1", "1om0", "1ot1", "1ot0", "1t1", "3om1", "3t1", "1om1"]
    inward = ["0m0", "0t0", "0m1", "0om0", "0ot1", "0ot0", "0t1", "2om1", "2t1", "0om1"]
    b_inner = ["3m0", "3m1", "2m0", "2t0", "2m1", "2om0", "2ot1", "2ot0", "3ot1", None]
    crossing = ["0m0", "0m1", "1m0", "1t0", "1m1", "1om0", "1ot1", "1ot0", "0ot1", None]
    y_outer = ["0om1", "0om0", "1om0", "0ot0", "2om0", "2om1", "2ot0", "3ot0", "3om1", "1om1"]
    x_outer = [None, None, "0ot1", "1t0", "2t0", "2t1", "1ot0", "2ot1", "3t1", "1t1"]
    y_inner = ["0om1", "0om0", None, "0ot0", "3om0", None, None, "2om1", None, None]
    x_inner = [None, None, "0ot1", None, None, "3t0", "3ot0", None, "2t1", None]

    def over_y(name):
        return name.replace("o", "")

    def over_x(name):
        return name.translate(str.maketrans("mt", "tm"))

    extra, sent = {}, []

    def settle():
        if len(sent) >= AHEAD:
            extra["sent"] = sent[-AHEAD]
        spots = [(u, k) for u in (at_outer, at_inner, extra) for k in u]
        unique = {id(u[k]): u[k] for u, k in spots}
        fresh = dict(zip(unique, lax.optimization_barrier(tuple(unique.values()))))
        for u, k in spots:
            u[k] = fresh[id(u[k])]

    def bring(value, pairs, *landings):
        got = send(value, pairs)
        sent.append(got)
        return [(units, name, got) for units, name in landings]

    landing = {}
    for r in range(1, 11):
        i = r - 1
        for units, name, value in landing.pop(r - 2, []):
            units[name] = value
        if r == 7:
            extra["in_a"], extra["keep_a"], extra["send_a"] = rotate("0", ["m0", "m1", "t0", "t1"], [], None, True)
        landing[r] = []
        if r == 10:
            acc_in, acc_out = rotate("123", ["m0"], [], None, False)
            extra["in_b"], extra["acc"] = rotate("123", ["t0"], [acc_in, acc_out], 0, False)
        for link in ORDER if r > 2 else "APQ":
            settle()
            if link == "A":
                value = pick(at_outer[inward[i]], at_inner[outward[i]])
                landing[r] += bring(value, group_pairs(link_a), (at_outer, a_outer[i]), (at_inner, a_inner[i]))
                continue
            over, from_outer, from_inner, around = (
                (over_y, y_outer[i], y_inner[i], lambda where: group_pairs([p for p in link_y if p[0] in where]))
                if link == "P"
                else (over_x, x_outer[i], x_inner[i], across_x)
            )
            spots, pairs, choices = [], [], []
            if from_outer:
                spots.append((at_outer, from_outer))
                choices.append(at_outer[over(from_outer)])
                pairs += around(at_ends)
            if from_inner:
                spots.append((at_inner, from_inner))
                choices.append(at_inner[over(from_inner)])
                pairs += around([c for c in cells if c not in at_ends])
            elif b_inner[i]:
                spots.append((at_inner, b_inner[i]))
                choices.append(at_inner[crossing[i]])
                pairs += group_pairs(link_b)
            landing[r] += bring(pick(choices[0], choices[-1]), pairs, *spots)

    block = jax.ShapeDtypeStruct((rows // 2, K), jnp.bfloat16)

    def squares(kernel, name, out_shape, *values):
        return pl.pallas_call(
            kernel,
            out_shape=out_shape,
            in_specs=[vmem] * len(values),
            out_specs=[vmem] * len(out_shape),
            compiler_params=pltpu.CompilerParams(vmem_limit_bytes=6 * 2**20),
            name=name,
        )(*values)

    def to_owner(k, value):
        return lax.ppermute(value, "dp", [(i, i ^ k) for i in range(8)]).astype(jnp.float32)

    in_a, keep_a, send_a = extra["in_a"], extra["keep_a"], extra["send_a"]
    in_b, acc = extra["in_b"], extra["acc"]
    rot_in, *near = squares(
        functools.partial(rotated_kernel, rows), "rotated",
        [jax.ShapeDtypeStruct((K, tokens), jnp.bfloat16)] + [block] * 2,
        in_a, swap_core(in_a), in_b, swap_core(in_b), keep_a, swap_core(send_a),
    )
    early = near[0].astype(jnp.float32) + to_owner(1, near[1])
    for units, name, value in landing.pop(9):
        units[name] = value
    keep_b, send_b = rotate("23", ["m1", "t1"], [acc], 2 * rows, True)
    far = squares(squares_kernel, "squares", [block] * 4, rot_in, keep_b, swap_core(send_b))
    for k in range(4):
        early = early + to_owner(4 + k, far[k])

    for units, name, value in landing.pop(10):
        units[name] = value
    keep_c, send_c = rotate("1", ["m1", "t1"], [acc], 0, True)
    early, come_c = lax.optimization_barrier((early, swap_core(send_c)))
    late = squares(squares_kernel, "squares", [block] * 2, rot_in, keep_c, come_c)
    total = early + to_owner(2, late[0]) + to_owner(3, late[1])
    return total * (1.0 / 8)


def solution(mesh):
    in_specs = (
        P(("group", "dp"), None, "basis"),
        P(("group", "dp"), None, "basis"),
        P("basis", "dp"),
        P("basis", "dp"),
    )
    out_specs = P(("group", "dp", "basis"), None)
    plane = (mesh.shape["group"], mesh.shape["dp"], mesh.shape["basis"]) == (2, 8, 2)
    return jax.shard_map(
        per_device_plane if plane else per_device_any,
        mesh=mesh,
        in_specs=in_specs,
        out_specs=out_specs,
        check_vma=False,
    )
```

```python
import functools

import jax
import jax.numpy as jnp
from jax import lax
from jax.experimental import pallas as pl
from jax.experimental.pallas import tpu as pltpu
from jax.sharding import PartitionSpec as P

TOK = 256
K = 384
LANES = 128
AHEAD = 30
ORDER = "APQ"
STEP = 5 * 10**8


def place_cols(left, piece):
    product = jnp.dot(left, piece, preferred_element_type=jnp.float32)
    return product


def per_device_any(activations, out_grads, input_basis, output_basis):
    acts = activations[0]
    grads = out_grads[0]
    tokens = acts.shape[0]
    part_in = place_cols(acts, lax.all_gather(input_basis, "dp", axis=1, tiled=True))
    part_out = place_cols(grads, lax.all_gather(output_basis, "dp", axis=1, tiled=True))
    rot_in = lax.psum(part_in, "basis").astype(jnp.bfloat16)
    data_count = lax.axis_size("dp")
    panel_count = lax.axis_size("basis")
    block = K // (data_count * panel_count)
    ordered = part_out.reshape(tokens, data_count, panel_count, block)
    ordered = jnp.transpose(ordered, (0, 2, 1, 3)).reshape(tokens, K)
    rot_out = lax.psum_scatter(ordered, "basis", scatter_dimension=1, tiled=True).astype(
        jnp.bfloat16
    )
    coeff = lax.dot_general(
        rot_out, rot_in, (((0,), (0,)), ((), ())), preferred_element_type=jnp.float32
    )
    coeff = coeff / jnp.sqrt(jnp.float32(TOK))
    summed = lax.psum_scatter(coeff * coeff, "dp", scatter_dimension=0, tiled=True)
    return summed / jnp.float32(data_count)


def nt_dot(left, right):
    return lax.dot_general(
        left, right, (((1,), (1,)), ((), ())), preferred_element_type=jnp.float32
    )


def pick_kernel(outer_ref, inner_ref, out_ref):
    z = lax.axis_index("dp") // 2
    outer = (z == 0) | (z == 3)

    @pl.when(outer)
    def _():
        out_ref[...] = outer_ref[...]

    @pl.when(jnp.logical_not(outer))
    def _():
        out_ref[...] = inner_ref[...]


def first_cut_kernel(in_ref, out_ref, m0, sems):
    x = lax.axis_index("group")
    in_half = in_ref.shape[1] // 2
    first = m0.shape[1] - in_half
    in_at = pl.multiple_of(x * in_half, LANES)
    out_at = pl.multiple_of(x * (out_ref.shape[1] // 2), LANES)
    ins = pltpu.make_async_copy(in_ref.at[:, pl.ds(in_at, in_half)], m0.at[:, :in_half], sems.at[0])
    outs = pltpu.make_async_copy(out_ref.at[:, pl.ds(out_at, first)], m0.at[:, in_half:], sems.at[1])
    ins.start()
    outs.start()
    ins.wait()
    outs.wait()


def cut_kernel(in_half, first, in_ref, out_ref, m1, t0, t1):
    x = lax.axis_index("group")
    out_half = first + m1.shape[1]
    for side, unit0, unit1 in ((x, None, m1), (1 - x, t0, t1)):
        in_at = pl.multiple_of(side * in_half, LANES)
        out_at = pl.multiple_of(side * out_half, LANES)
        next_at = pl.multiple_of(side * out_half + first, LANES)
        if unit0 is not None:
            unit0[:, :in_half] = in_ref[:, pl.ds(in_at, in_half)]
            unit0[:, in_half:] = out_ref[:, pl.ds(out_at, first)]
        unit1[...] = out_ref[:, pl.ds(next_at, unit1.shape[1])]


def rotate_kernel(plan, in_half, first, acts_ref, grads_ref, *refs):
    x = lax.axis_index("group")
    core = lax.axis_index("basis")
    terms, acc_from, last = plan
    refs = list(refs)
    stack = refs.pop()
    z = lax.axis_index("dp") // 2
    outer = (z == 0) | (z == 3)
    out_half = grads_ref.shape[1] // 2
    rot_in = rot_out = None
    for mine, index, pieces in terms:
        rows = refs[0].shape[0]
        for i, (at_outer, at_inner) in enumerate(pieces):
            at = slice(i * rows, (i + 1) * rows)
            if at_outer == at_inner:
                stack[at] = refs[at_outer][...]
                continue

            @pl.when(outer)
            def _():
                stack[at] = refs[at_outer][...]

            @pl.when(jnp.logical_not(outer))
            def _():
                stack[at] = refs[at_inner][...]

        side = x if mine else 1 - x
        if index == 0:
            cols = pl.ds(pl.multiple_of(side * in_half, LANES), in_half)
            part = nt_dot(stack[:, :in_half], acts_ref[:, cols])
            rot_in = part if rot_in is None else rot_in + part
            cols = pl.ds(pl.multiple_of(side * out_half, LANES), first)
            part = nt_dot(stack[:, in_half:], grads_ref[:, cols])
        else:
            cols = pl.ds(pl.multiple_of(side * out_half + first, LANES), out_half - first)
            part = nt_dot(stack[...], grads_ref[:, cols])
        rot_out = part if rot_out is None else rot_out + part
    panel = refs[0].shape[0] // 2
    refs = refs[1 + max(i for term in terms for pair in term[2] for i in pair) :]
    if acc_from is not None:
        at = slice(acc_from, acc_from + rot_out.shape[0])
        if rot_in is not None:
            rot_in += refs.pop(0)[at]
        rot_out += refs.pop(0)[at]
    if rot_in is not None:
        refs.pop(0)[...] = rot_in
    if not last:
        refs.pop(0)[...] = rot_out
        return
    keep, send = refs
    for shard in range(rot_out.shape[0] // (2 * panel)):
        low = rot_out[2 * shard * panel : (2 * shard + 1) * panel]
        high = rot_out[(2 * shard + 1) * panel : 2 * (shard + 1) * panel]
        at = slice(shard * panel, (shard + 1) * panel)
        keep[at] = jnp.where(core == 0, low, high)
        send[at] = jnp.where(core == 0, high, low)


def store_squares(keep, come, rot_in, outs):
    rot_out = (keep[...] + come[...]).astype(jnp.bfloat16)
    coeff = nt_dot(rot_out, rot_in) * (1.0 / TOK**0.5)
    square = coeff * coeff
    panel = outs[0].shape[0]
    for block, ref in enumerate(outs):
        ref[...] = square[block * panel : (block + 1) * panel].astype(ref.dtype)


def rotated_kernel(rows, in_a, in_a2, in_b, in_b2, keep, come, in_ref, *outs):
    me = lax.axis_index("dp")
    for block in range(8):
        at = pl.ds((block if block < 2 else block - 2) * rows, rows)
        total = in_a[at] + in_a2[at] if block < 2 else in_b[at] + in_b2[at]
        begin = pl.multiple_of((me ^ block) * rows, 16)
        in_ref[pl.ds(begin, rows), :] = total.astype(jnp.bfloat16)
    store_squares(keep, come, in_ref[...], outs)


def squares_kernel(in_ref, keep, come, *outs):
    store_squares(keep, come, in_ref[...], outs)


def per_device_plane(activations, out_grads, input_basis, output_basis):
    acts, grads = activations[0], out_grads[0]
    in_t, out_t = input_basis.T, output_basis.T
    rows = in_t.shape[0]
    tokens = acts.shape[0]
    me = lax.axis_index("dp")
    z, y = me // 2, me % 2
    in_half = in_t.shape[1] // 2
    width = (in_t.shape[1] + out_t.shape[1]) // 4
    first = width - in_half

    vmem = pl.BlockSpec(memory_space=pltpu.VMEM)

    def swap_core(value):
        return lax.ppermute(value, "basis", [(0, 1), (1, 0)])

    unit = jax.ShapeDtypeStruct((rows, width), in_t.dtype)
    m0 = pl.pallas_call(
        first_cut_kernel,
        out_shape=unit,
        in_specs=[pl.BlockSpec(memory_space=pltpu.HBM)] * 2,
        out_specs=vmem,
        scratch_shapes=[pltpu.SemaphoreType.DMA((2,))],
        compiler_params=pltpu.CompilerParams(vmem_limit_bytes=62 * 2**20),
        name="first_cut",
    )(in_t, out_t)
    m1, t0, t1 = pl.pallas_call(
        functools.partial(cut_kernel, in_half, first),
        out_shape=[unit] * 3,
        in_specs=[vmem] * 2,
        out_specs=[vmem] * 3,
        compiler_params=pltpu.CompilerParams(vmem_limit_bytes=8 * 2**20),
        name="cut",
    )(in_t, out_t)

    def rotate(slots, names, acc, acc_from, last):
        terms, pieces, out_shape = [], [], []
        count = 2 * len(slots)

        def ref_of(value):
            for i, piece in enumerate(pieces):
                if piece is value:
                    return i
            pieces.append(value)
            return len(pieces) - 1

        for name in names:
            terms.append((name[0] == "m", int(name[1]), [
                (ref_of(at_outer[s + k]), ref_of(at_inner[s + k])) for s in slots for k in (name, "o" + name)
            ]))
        full = jax.ShapeDtypeStruct((count * rows, tokens), jnp.float32)
        panel = jax.ShapeDtypeStruct((count * rows // 2, tokens), jnp.float32)
        if any(name[1] == "0" for name in names):
            out_shape.append(full)
        out_shape += [panel, panel] if last else [full]
        return pl.pallas_call(
            functools.partial(rotate_kernel, (terms, acc_from, last), in_half, first),
            out_shape=out_shape,
            in_specs=[vmem] * (2 + len(pieces) + len(acc)),
            out_specs=[vmem] * len(out_shape),
            scratch_shapes=[pltpu.VMEM((count * rows, width), in_t.dtype)],
            compiler_params=pltpu.CompilerParams(vmem_limit_bytes=20 * 2**20),
            cost_estimate=pl.CostEstimate(
                flops=2 * len(names) * count * rows * width * tokens,
                bytes_accessed=2 * len(pieces) * rows * width,
                transcendentals=0,
            ),
            name="rotate",
        )(acts, grads, *pieces, *acc)

    outer = (z == 0) | (z == 3)
    cells = range(8)
    link_a = [(i, i ^ 2) for i in cells]
    link_b = [(i, 2 * (3 - i // 2) + i % 2) for i in cells if 2 <= i < 6]
    link_y = [(i, i ^ 1) for i in cells]
    at_ends = [i for i in cells if i < 2 or i >= 6]

    def group_pairs(pairs):
        return [(8 * g + a, 8 * g + b) for g in range(2) for a, b in pairs]

    def across_x(where):
        return [(8 * g + i, 8 * (1 - g) + i) for g in range(2) for i in where]

    def send(value, pairs):
        return lax.ppermute(value, ("group", "dp"), pairs)

    def pick(for_outer, for_inner):
        if for_outer is for_inner:
            return for_outer
        return pl.pallas_call(
            pick_kernel,
            out_shape=unit,
            in_specs=[vmem] * 2,
            out_specs=vmem,
            compiler_params=pltpu.CompilerParams(vmem_limit_bytes=4 * 2**20),
            cost_estimate=pl.CostEstimate(flops=STEP, bytes_accessed=8192, transcendentals=0),
            name="pick",
        )(for_outer, for_inner)

    at_outer = {"0m0": m0, "0m1": m1, "0t0": t0, "0t1": t1}
    at_inner = dict(at_outer)
    a_outer = ["1m0", "1m1", "2m0", "2m1", "3m0", "3t0", "3m1", "3om0", "3ot1", "1ot1"]
    outward = ["0m0", "0m1", "3m0", "3m1", "2m0", "2t0", "2m1", "2om0", "2ot1", "0ot1"]
    a_inner = ["1m0", "1t0", "1m1", "1om0", "1ot1", "1ot0", "1t1", "3om1", "3t1", "1om1"]
    inward = ["0m0", "0t0", "0m1", "0om0", "0ot1", "0ot0", "0t1", "2om1", "2t1", "0om1"]
    b_inner = ["3m0", "3m1", "2m0", "2t0", "2m1", "2om0", "2ot1", "2ot0", "3ot1", None]
    crossing = ["0m0", "0m1", "1m0", "1t0", "1m1", "1om0", "1ot1", "1ot0", "0ot1", None]
    y_outer = ["0om1", "0om0", "1om0", "0ot0", "2om0", "2om1", "2ot0", "3ot0", "3om1", "1om1"]
    x_outer = [None, None, "0ot1", "1t0", "2t0", "2t1", "1ot0", "2ot1", "3t1", "1t1"]
    y_inner = ["0om1", "0om0", None, "0ot0", "3om0", None, None, "2om1", None, None]
    x_inner = [None, None, "0ot1", None, None, "3t0", "3ot0", None, "2t1", None]

    def over_y(name):
        return name.replace("o", "")

    def over_x(name):
        return name.translate(str.maketrans("mt", "tm"))

    extra, sent = {}, []

    def settle():
        if len(sent) >= AHEAD:
            extra["sent"] = sent[-AHEAD]
        spots = [(u, k) for u in (at_outer, at_inner, extra) for k in u]
        unique = {id(u[k]): u[k] for u, k in spots}
        fresh = dict(zip(unique, lax.optimization_barrier(tuple(unique.values()))))
        for u, k in spots:
            u[k] = fresh[id(u[k])]

    def bring(value, pairs, *landings):
        got = send(value, pairs)
        sent.append(got)
        return [(units, name, got) for units, name in landings]

    landing = {}
    for r in range(1, 11):
        i = r - 1
        for units, name, value in landing.pop(r - 2, []):
            units[name] = value
        if r == 7:
            extra["in_a"], extra["keep_a"], extra["send_a"] = rotate("0", ["m0", "m1", "t0", "t1"], [], None, True)
        landing[r] = []
        if r == 10:
            acc_in, acc_out = rotate("123", ["m0"], [], None, False)
            extra["in_b"], extra["acc"] = rotate("123", ["t0"], [acc_in, acc_out], 0, False)
        for link in ORDER if r > 2 else "APQ":
            settle()
            if link == "A":
                value = pick(at_outer[inward[i]], at_inner[outward[i]])
                landing[r] += bring(value, group_pairs(link_a), (at_outer, a_outer[i]), (at_inner, a_inner[i]))
                continue
            over, from_outer, from_inner, around = (
                (over_y, y_outer[i], y_inner[i], lambda where: group_pairs([p for p in link_y if p[0] in where]))
                if link == "P"
                else (over_x, x_outer[i], x_inner[i], across_x)
            )
            spots, pairs, choices = [], [], []
            if from_outer:
                spots.append((at_outer, from_outer))
                choices.append(at_outer[over(from_outer)])
                pairs += around(at_ends)
            if from_inner:
                spots.append((at_inner, from_inner))
                choices.append(at_inner[over(from_inner)])
                pairs += around([c for c in cells if c not in at_ends])
            elif b_inner[i]:
                spots.append((at_inner, b_inner[i]))
                choices.append(at_inner[crossing[i]])
                pairs += group_pairs(link_b)
            landing[r] += bring(pick(choices[0], choices[-1]), pairs, *spots)

    block = jax.ShapeDtypeStruct((rows // 2, K), jnp.bfloat16)

    def squares(kernel, name, out_shape, *values):
        return pl.pallas_call(
            kernel,
            out_shape=out_shape,
            in_specs=[vmem] * len(values),
            out_specs=[vmem] * len(out_shape),
            compiler_params=pltpu.CompilerParams(vmem_limit_bytes=6 * 2**20),
            name=name,
        )(*values)

    def to_owner(k, value):
        return lax.ppermute(value, "dp", [(i, i ^ k) for i in range(8)]).astype(jnp.float32)

    in_a, keep_a, send_a = extra["in_a"], extra["keep_a"], extra["send_a"]
    in_b, acc = extra["in_b"], extra["acc"]
    rot_in, *near = squares(
        functools.partial(rotated_kernel, rows), "rotated",
        [jax.ShapeDtypeStruct((K, tokens), jnp.bfloat16)] + [block] * 2,
        in_a, swap_core(in_a), in_b, swap_core(in_b), keep_a, swap_core(send_a),
    )
    for units, name, value in landing.pop(9):
        units[name] = value
    keep_b, send_b = rotate("23", ["m1", "t1"], [acc], 2 * rows, True)
    far = squares(squares_kernel, "squares", [block] * 4, rot_in, keep_b, swap_core(send_b))
    waiting = {1: near[1], 4: far[0], 5: far[1], 6: far[2], 7: far[3]}
    early = near[0].astype(jnp.float32)
    for k in (6, 7):
        early = early + to_owner(k, waiting[k])

    for units, name, value in landing.pop(10):
        units[name] = value
    keep_c, send_c = rotate("1", ["m1", "t1"], [acc], 0, True)
    early, come_c = lax.optimization_barrier((early, swap_core(send_c)))
    late = squares(squares_kernel, "squares", [block] * 2, rot_in, keep_c, come_c)
    total = early + to_owner(2, late[0]) + to_owner(3, late[1])
    for k in (1, 4, 5):
        total = total + to_owner(k, waiting[k])
    return total * (1.0 / 8)


def solution(mesh):
    in_specs = (
        P(("group", "dp"), None, "basis"),
        P(("group", "dp"), None, "basis"),
        P("basis", "dp"),
        P("basis", "dp"),
    )
    out_specs = P(("group", "dp", "basis"), None)
    plane = (mesh.shape["group"], mesh.shape["dp"], mesh.shape["basis"]) == (2, 8, 2)
    return jax.shard_map(
        per_device_plane if plane else per_device_any,
        mesh=mesh,
        in_specs=in_specs,
        out_specs=out_specs,
        check_vma=False,
    )
```

```python
import functools

import jax
import jax.numpy as jnp
from jax import lax
from jax.experimental import pallas as pl
from jax.experimental.pallas import tpu as pltpu
from jax.sharding import PartitionSpec as P

TOK = 256
K = 384
LANES = 128
AHEAD = 30
ORDER = "APQ"
STEP = 5 * 10**8


def place_cols(left, piece):
    product = jnp.dot(left, piece, preferred_element_type=jnp.float32)
    return product


def per_device_any(activations, out_grads, input_basis, output_basis):
    acts = activations[0]
    grads = out_grads[0]
    tokens = acts.shape[0]
    part_in = place_cols(acts, lax.all_gather(input_basis, "dp", axis=1, tiled=True))
    part_out = place_cols(grads, lax.all_gather(output_basis, "dp", axis=1, tiled=True))
    rot_in = lax.psum(part_in, "basis").astype(jnp.bfloat16)
    data_count = lax.axis_size("dp")
    panel_count = lax.axis_size("basis")
    block = K // (data_count * panel_count)
    ordered = part_out.reshape(tokens, data_count, panel_count, block)
    ordered = jnp.transpose(ordered, (0, 2, 1, 3)).reshape(tokens, K)
    rot_out = lax.psum_scatter(ordered, "basis", scatter_dimension=1, tiled=True).astype(
        jnp.bfloat16
    )
    coeff = lax.dot_general(
        rot_out, rot_in, (((0,), (0,)), ((), ())), preferred_element_type=jnp.float32
    )
    coeff = coeff / jnp.sqrt(jnp.float32(TOK))
    summed = lax.psum_scatter(coeff * coeff, "dp", scatter_dimension=0, tiled=True)
    return summed / jnp.float32(data_count)


def nt_dot(left, right):
    return lax.dot_general(
        left, right, (((1,), (1,)), ((), ())), preferred_element_type=jnp.float32
    )


def pick_kernel(outer_ref, inner_ref, out_ref):
    z = lax.axis_index("dp") // 2
    outer = (z == 0) | (z == 3)

    @pl.when(outer)
    def _():
        out_ref[...] = outer_ref[...]

    @pl.when(jnp.logical_not(outer))
    def _():
        out_ref[...] = inner_ref[...]


def first_cut_kernel(in_ref, out_ref, m0, sems):
    x = lax.axis_index("group")
    in_half = in_ref.shape[1] // 2
    first = m0.shape[1] - in_half
    in_at = pl.multiple_of(x * in_half, LANES)
    out_at = pl.multiple_of(x * (out_ref.shape[1] // 2), LANES)
    ins = pltpu.make_async_copy(in_ref.at[:, pl.ds(in_at, in_half)], m0.at[:, :in_half], sems.at[0])
    outs = pltpu.make_async_copy(out_ref.at[:, pl.ds(out_at, first)], m0.at[:, in_half:], sems.at[1])
    ins.start()
    outs.start()
    ins.wait()
    outs.wait()


def cut_kernel(in_half, first, in_ref, out_ref, m1, t0, t1):
    x = lax.axis_index("group")
    out_half = first + m1.shape[1]
    for side, unit0, unit1 in ((x, None, m1), (1 - x, t0, t1)):
        in_at = pl.multiple_of(side * in_half, LANES)
        out_at = pl.multiple_of(side * out_half, LANES)
        next_at = pl.multiple_of(side * out_half + first, LANES)
        if unit0 is not None:
            unit0[:, :in_half] = in_ref[:, pl.ds(in_at, in_half)]
            unit0[:, in_half:] = out_ref[:, pl.ds(out_at, first)]
        unit1[...] = out_ref[:, pl.ds(next_at, unit1.shape[1])]


def rotate_kernel(plan, in_half, first, acts_ref, grads_ref, *refs):
    x = lax.axis_index("group")
    core = lax.axis_index("basis")
    terms, acc_from, last = plan
    refs = list(refs)
    stack = refs.pop()
    z = lax.axis_index("dp") // 2
    outer = (z == 0) | (z == 3)
    out_half = grads_ref.shape[1] // 2
    rot_in = rot_out = None
    for mine, index, pieces in terms:
        rows = refs[0].shape[0]
        for i, (at_outer, at_inner) in enumerate(pieces):
            at = slice(i * rows, (i + 1) * rows)
            if at_outer == at_inner:
                stack[at] = refs[at_outer][...]
                continue

            @pl.when(outer)
            def _():
                stack[at] = refs[at_outer][...]

            @pl.when(jnp.logical_not(outer))
            def _():
                stack[at] = refs[at_inner][...]

        side = x if mine else 1 - x
        if index == 0:
            cols = pl.ds(pl.multiple_of(side * in_half, LANES), in_half)
            part = nt_dot(stack[:, :in_half], acts_ref[:, cols])
            rot_in = part if rot_in is None else rot_in + part
            cols = pl.ds(pl.multiple_of(side * out_half, LANES), first)
            part = nt_dot(stack[:, in_half:], grads_ref[:, cols])
        else:
            cols = pl.ds(pl.multiple_of(side * out_half + first, LANES), out_half - first)
            part = nt_dot(stack[...], grads_ref[:, cols])
        rot_out = part if rot_out is None else rot_out + part
    panel = refs[0].shape[0] // 2
    refs = refs[1 + max(i for term in terms for pair in term[2] for i in pair) :]
    if acc_from is not None:
        at = slice(acc_from, acc_from + rot_out.shape[0])
        if rot_in is not None:
            rot_in += refs.pop(0)[at]
        rot_out += refs.pop(0)[at]
    if rot_in is not None:
        refs.pop(0)[...] = rot_in
    if not last:
        refs.pop(0)[...] = rot_out
        return
    keep, send = refs
    for shard in range(rot_out.shape[0] // (2 * panel)):
        low = rot_out[2 * shard * panel : (2 * shard + 1) * panel]
        high = rot_out[(2 * shard + 1) * panel : 2 * (shard + 1) * panel]
        at = slice(shard * panel, (shard + 1) * panel)
        keep[at] = jnp.where(core == 0, low, high)
        send[at] = jnp.where(core == 0, high, low)


def store_squares(keep, come, rot_in, outs):
    rot_out = (keep[...] + come[...]).astype(jnp.bfloat16)
    coeff = nt_dot(rot_out, rot_in) * (1.0 / TOK**0.5)
    square = coeff * coeff
    panel = outs[0].shape[0]
    for block, ref in enumerate(outs):
        ref[...] = square[block * panel : (block + 1) * panel].astype(ref.dtype)


def rotated_kernel(rows, in_a, in_a2, in_b, in_b2, keep, come, in_ref, *outs):
    me = lax.axis_index("dp")
    for block in range(8):
        at = pl.ds((block if block < 2 else block - 2) * rows, rows)
        total = in_a[at] + in_a2[at] if block < 2 else in_b[at] + in_b2[at]
        begin = pl.multiple_of((me ^ block) * rows, 16)
        in_ref[pl.ds(begin, rows), :] = total.astype(jnp.bfloat16)
    store_squares(keep, come, in_ref[...], outs)


def squares_kernel(in_ref, keep, come, *outs):
    store_squares(keep, come, in_ref[...], outs)


def per_device_plane(activations, out_grads, input_basis, output_basis):
    acts, grads = activations[0], out_grads[0]
    in_t, out_t = input_basis.T, output_basis.T
    rows = in_t.shape[0]
    tokens = acts.shape[0]
    me = lax.axis_index("dp")
    z, y = me // 2, me % 2
    in_half = in_t.shape[1] // 2
    width = (in_t.shape[1] + out_t.shape[1]) // 4
    first = width - in_half

    vmem = pl.BlockSpec(memory_space=pltpu.VMEM)

    def swap_core(value):
        return lax.ppermute(value, "basis", [(0, 1), (1, 0)])

    unit = jax.ShapeDtypeStruct((rows, width), in_t.dtype)
    m0 = pl.pallas_call(
        first_cut_kernel,
        out_shape=unit,
        in_specs=[pl.BlockSpec(memory_space=pltpu.HBM)] * 2,
        out_specs=vmem,
        scratch_shapes=[pltpu.SemaphoreType.DMA((2,))],
        compiler_params=pltpu.CompilerParams(vmem_limit_bytes=62 * 2**20),
        name="first_cut",
    )(in_t, out_t)
    m1, t0, t1 = pl.pallas_call(
        functools.partial(cut_kernel, in_half, first),
        out_shape=[unit] * 3,
        in_specs=[vmem] * 2,
        out_specs=[vmem] * 3,
        compiler_params=pltpu.CompilerParams(vmem_limit_bytes=8 * 2**20),
        name="cut",
    )(in_t, out_t)

    def rotate(slots, names, acc, acc_from, last):
        terms, pieces, out_shape = [], [], []
        count = 2 * len(slots)

        def ref_of(value):
            for i, piece in enumerate(pieces):
                if piece is value:
                    return i
            pieces.append(value)
            return len(pieces) - 1

        for name in names:
            terms.append((name[0] == "m", int(name[1]), [
                (ref_of(at_outer[s + k]), ref_of(at_inner[s + k])) for s in slots for k in (name, "o" + name)
            ]))
        full = jax.ShapeDtypeStruct((count * rows, tokens), jnp.float32)
        panel = jax.ShapeDtypeStruct((count * rows // 2, tokens), jnp.float32)
        if any(name[1] == "0" for name in names):
            out_shape.append(full)
        out_shape += [panel, panel] if last else [full]
        return pl.pallas_call(
            functools.partial(rotate_kernel, (terms, acc_from, last), in_half, first),
            out_shape=out_shape,
            in_specs=[vmem] * (2 + len(pieces) + len(acc)),
            out_specs=[vmem] * len(out_shape),
            scratch_shapes=[pltpu.VMEM((count * rows, width), in_t.dtype)],
            compiler_params=pltpu.CompilerParams(vmem_limit_bytes=20 * 2**20),
            cost_estimate=pl.CostEstimate(
                flops=2 * len(names) * count * rows * width * tokens,
                bytes_accessed=2 * len(pieces) * rows * width,
                transcendentals=0,
            ),
            name="rotate",
        )(acts, grads, *pieces, *acc)

    outer = (z == 0) | (z == 3)
    cells = range(8)
    link_a = [(i, i ^ 2) for i in cells]
    link_b = [(i, 2 * (3 - i // 2) + i % 2) for i in cells if 2 <= i < 6]
    link_y = [(i, i ^ 1) for i in cells]
    at_ends = [i for i in cells if i < 2 or i >= 6]

    def group_pairs(pairs):
        return [(8 * g + a, 8 * g + b) for g in range(2) for a, b in pairs]

    def across_x(where):
        return [(8 * g + i, 8 * (1 - g) + i) for g in range(2) for i in where]

    def send(value, pairs):
        return lax.ppermute(value, ("group", "dp"), pairs)

    def pick(for_outer, for_inner):
        if for_outer is for_inner:
            return for_outer
        return pl.pallas_call(
            pick_kernel,
            out_shape=unit,
            in_specs=[vmem] * 2,
            out_specs=vmem,
            compiler_params=pltpu.CompilerParams(vmem_limit_bytes=4 * 2**20),
            cost_estimate=pl.CostEstimate(flops=STEP, bytes_accessed=8192, transcendentals=0),
            name="pick",
        )(for_outer, for_inner)

    at_outer = {"0m0": m0, "0m1": m1, "0t0": t0, "0t1": t1}
    at_inner = dict(at_outer)
    a_outer = ["1m0", "1m1", "2m0", "2m1", "3m0", "3t0", "3m1", "3om0", "3ot1", "1ot1"]
    outward = ["0m0", "0m1", "3m0", "3m1", "2m0", "2t0", "2m1", "2om0", "2ot1", "0ot1"]
    a_inner = ["1m0", "1t0", "1m1", "1om0", "1ot1", "1ot0", "1t1", "3om1", "3t1", "1om1"]
    inward = ["0m0", "0t0", "0m1", "0om0", "0ot1", "0ot0", "0t1", "2om1", "2t1", "0om1"]
    b_inner = ["3m0", "3m1", "2m0", "2t0", "2m1", "2om0", "2ot1", "2ot0", "3ot1", None]
    crossing = ["0m0", "0m1", "1m0", "1t0", "1m1", "1om0", "1ot1", "1ot0", "0ot1", None]
    y_outer = ["0om1", "0om0", "1om0", "0ot0", "2om0", "2om1", "2ot0", "3ot0", "3om1", "1om1"]
    x_outer = [None, None, "0ot1", "1t0", "2t0", "2t1", "1ot0", "2ot1", "3t1", "1t1"]
    y_inner = ["0om1", "0om0", None, "0ot0", "3om0", None, None, "2om1", None, None]
    x_inner = [None, None, "0ot1", None, None, "3t0", "3ot0", None, "2t1", None]

    def over_y(name):
        return name.replace("o", "")

    def over_x(name):
        return name.translate(str.maketrans("mt", "tm"))

    extra, sent = {}, []

    def settle():
        if len(sent) >= AHEAD:
            extra["sent"] = sent[-AHEAD]
        spots = [(u, k) for u in (at_outer, at_inner, extra) for k in u]
        unique = {id(u[k]): u[k] for u, k in spots}
        fresh = dict(zip(unique, lax.optimization_barrier(tuple(unique.values()))))
        for u, k in spots:
            u[k] = fresh[id(u[k])]

    def bring(value, pairs, *landings):
        got = send(value, pairs)
        sent.append(got)
        return [(units, name, got) for units, name in landings]

    landing = {}
    for r in range(1, 11):
        i = r - 1
        for units, name, value in landing.pop(r - 2, []):
            units[name] = value
        if r == 7:
            extra["in_a"], extra["keep_a"], extra["send_a"] = rotate("0", ["m0", "m1", "t0", "t1"], [], None, True)
        landing[r] = []
        if r == 10:
            acc_in, acc_out = rotate("123", ["m0"], [], None, False)
            extra["in_b"], extra["acc"] = rotate("123", ["t0"], [acc_in, acc_out], 0, False)
        for link in ORDER if r > 2 else "APQ":
            settle()
            if link == "A":
                value = pick(at_outer[inward[i]], at_inner[outward[i]])
                landing[r] += bring(value, group_pairs(link_a), (at_outer, a_outer[i]), (at_inner, a_inner[i]))
                continue
            over, from_outer, from_inner, around = (
                (over_y, y_outer[i], y_inner[i], lambda where: group_pairs([p for p in link_y if p[0] in where]))
                if link == "P"
                else (over_x, x_outer[i], x_inner[i], across_x)
            )
            spots, pairs, choices = [], [], []
            if from_outer:
                spots.append((at_outer, from_outer))
                choices.append(at_outer[over(from_outer)])
                pairs += around(at_ends)
            if from_inner:
                spots.append((at_inner, from_inner))
                choices.append(at_inner[over(from_inner)])
                pairs += around([c for c in cells if c not in at_ends])
            elif b_inner[i]:
                spots.append((at_inner, b_inner[i]))
                choices.append(at_inner[crossing[i]])
                pairs += group_pairs(link_b)
            landing[r] += bring(pick(choices[0], choices[-1]), pairs, *spots)

    block = jax.ShapeDtypeStruct((rows // 2, K), jnp.bfloat16)

    def squares(kernel, name, out_shape, *values):
        return pl.pallas_call(
            kernel,
            out_shape=out_shape,
            in_specs=[vmem] * len(values),
            out_specs=[vmem] * len(out_shape),
            compiler_params=pltpu.CompilerParams(vmem_limit_bytes=6 * 2**20),
            name=name,
        )(*values)

    def to_owner(k, value):
        return lax.ppermute(value, "dp", [(i, i ^ k) for i in range(8)]).astype(jnp.float32)

    in_a, keep_a, send_a = extra["in_a"], extra["keep_a"], extra["send_a"]
    in_b, acc = extra["in_b"], extra["acc"]
    rot_in, *near = squares(
        functools.partial(rotated_kernel, rows), "rotated",
        [jax.ShapeDtypeStruct((K, tokens), jnp.bfloat16)] + [block] * 2,
        in_a, swap_core(in_a), in_b, swap_core(in_b), keep_a, swap_core(send_a),
    )
    for units, name, value in landing.pop(9):
        units[name] = value
    keep_b, send_b = rotate("23", ["m1", "t1"], [acc], 2 * rows, True)
    far = squares(squares_kernel, "squares", [block] * 4, rot_in, keep_b, swap_core(send_b))
    waiting = {6: far[2], 7: far[3]}
    early = near[0].astype(jnp.float32)
    for k in (6, 7):
        early = early + to_owner(k, waiting[k])

    for units, name, value in landing.pop(10):
        units[name] = value
    keep_c, send_c = rotate("1", ["m1", "t1"], [acc], 0, True)
    early, come_c = lax.optimization_barrier((early, swap_core(send_c)))
    late = squares(squares_kernel, "squares", [block] * 2, rot_in, keep_c, come_c)
    total = early + to_owner(2, late[0]) + to_owner(3, late[1])
    got = to_owner(1, jnp.concatenate([near[1], far[1]], axis=0))
    half = rows // 2
    total = total + got[:half] + to_owner(4, far[0].astype(jnp.float32) + got[half:])
    return total * (1.0 / 8)


def solution(mesh):
    in_specs = (
        P(("group", "dp"), None, "basis"),
        P(("group", "dp"), None, "basis"),
        P("basis", "dp"),
        P("basis", "dp"),
    )
    out_specs = P(("group", "dp", "basis"), None)
    plane = (mesh.shape["group"], mesh.shape["dp"], mesh.shape["basis"]) == (2, 8, 2)
    return jax.shard_map(
        per_device_plane if plane else per_device_any,
        mesh=mesh,
        in_specs=in_specs,
        out_specs=out_specs,
        check_vma=False,
    )
```
